32 devices in a mesh: groups: 2 (over y), virt: 4 (over z), pair: 2 (over x), sub: 2 (over core).
Axes of the slice: x: 2, y: 2, z: 4, core: 2. Of those that a mesh axis runs over, the one named last changes fastest.
Arguments:
- amplitudes: bfloat16 [3840, 2048], P(('groups', 'pair', 'virt'), 'sub'), parts along dimension 0, may hold values from -4 to 4
- driver: bfloat16 [3840, 2048], P(('groups', 'pair', 'virt'), 'sub'), parts along dimension 0, may hold values from -6 to 6
- integrals: bfloat16 [4096, 2048], P(('groups', 'sub'), 'virt'), parts along dimension 0, may hold values from -0.125 to 0.125
- pair_energy: float32 [3840], P(('groups', 'pair', 'virt')), parts along dimension 0, may hold values from -1.5 to -0.5
- col_energy: float32 [4096], P(('groups', 'sub')), parts along dimension 0, may hold values from 0.5 to 3
- tile_irrep: int32 [32], P(('groups', 'sub')), parts along dimension 0, may hold values from 0 to 3
- pair_irrep: int32 [3840], P(('groups', 'pair', 'virt')), parts along dimension 0, may hold values from 0 to 3, as said below
- mirror_slot: int32 [3840], P(('groups', 'pair', 'virt')), parts along dimension 0, may hold values from 0 to 239, as said below
Outputs:
- amplitudes_next: float32 [3840, 2048], P(('groups', 'pair', 'virt'), 'sub'), parts along dimension 0
The draws below stay inside these ranges and needn't reach their ends.
There are 2 independent parts, one for each index of `groups`. The reference program is written for one: setup_inputs(seed, part) draws one part's arguments, and reference() takes and returns one part's arrays. A program takes and returns all parts, laid end to end along the dimension named above; each array names one. Nothing has to cross between parts.
Inputs may be any that keep to these rules, and one draw needn't show every extreme that they name: `mirror_slot`: within each pair of mirrored blocks (block b and block b + 4) the map is a permutation whose entries point back to each other. `pair_irrep`: A pair and its mirror carry the same label.
All inputs are finite; a program needn't handle non-finite values.
Results may differ from the reference program's by a relative error of at most 0.00088.
Values may be sent and summed in bfloat16 or wider, within the bound.
No kernel may reach another device: no remote copies, remote signals or barrier semaphores. Data moves between devices by JAX's collectives and lax.ppermute only.
A program may use at most 64 MiB of HBM per device.

```python
import jax
import jax.numpy as jnp

ROWS_DEV = 240
NVP = 2048
ITERS = 2
IRREPS = 4
PAIRS = 1920


def mirror_tables(key):
    block_count = PAIRS // ROWS_DEV
    half_blocks = block_count // 2
    subkeys = jax.random.split(key, half_blocks)
    permuted = jax.vmap(lambda subkey_one: jax.random.permutation(subkey_one, ROWS_DEV))(subkeys).astype(jnp.int32)
    inverse = jnp.argsort(permuted, axis=1, stable=True).astype(jnp.int32)
    labels = jax.random.randint(jax.random.fold_in(key, 7), (half_blocks, ROWS_DEV), 0, IRREPS).astype(jnp.int32)
    return (permuted, inverse, labels)


def draw_mirror_slot(key, part):
    permuted, inverse, labels = mirror_tables(key)
    return jnp.concatenate([permuted, inverse], axis=0).reshape(PAIRS)


def draw_pair_irrep(key, part):
    permuted, inverse, labels = mirror_tables(key)
    labels_back = jnp.take_along_axis(labels, inverse, axis=1)
    return jnp.concatenate([labels, labels_back], axis=0).reshape(PAIRS)


def place_ends(array, rng, least, largest):
    longest = array.shape.index(max(array.shape))
    spots = []
    for shift in (0, 1):
        where = [jax.random.randint(jax.random.fold_in(rng, axis), (), 0, length) for axis, length in enumerate(array.shape)]
        where[longest] = (where[longest] + shift) % array.shape[longest]
        spots.append(tuple(where))
    return array.at[spots[0]].set(least).at[spots[1]].set(largest)


def block_scale(stream_key, dims, cuts, low, high):
    loudness, own = 1.0, jax.random.fold_in(stream_key, 6)
    for dim, blocks in cuts:
        steps = jnp.exp(jax.random.uniform(jax.random.fold_in(own, dim), (blocks,), jnp.float32, low / len(cuts), high / len(cuts)))
        loudness = loudness * jnp.repeat(steps, dims[dim] // blocks).reshape([-1 if axis == dim else 1 for axis in range(len(dims))])
    return loudness


def normal_values(key, dims, width, most, pieces=(), kind=jnp.bfloat16):
    result = width * jax.random.normal(key, dims, jnp.float32)
    if pieces:
        result = result * block_scale(key, dims, pieces, -0.22, 0.18)
    return jnp.clip(result, -most, most).astype(kind)


def setup_inputs(seed: int = 0, part: int = 0) -> dict:
    key_of = jax.random.split(jax.random.key(seed), 9)
    part_keys = jax.random.split(jax.random.fold_in(key_of[8], part), 9)
    return {
        "amplitudes": normal_values(part_keys[0], (PAIRS, NVP), 0.5, 4.0, ((0, 8), (1, 2))),
        "driver": normal_values(part_keys[1], (PAIRS, NVP), 1.0, 6.0, ((0, 8), (1, 2))),
        "integrals": normal_values(part_keys[2], (NVP, NVP), NVP ** -0.5, 0.125, ((0, 2), (1, 4))),
        "pair_energy": jnp.clip(-1.5 + 1.0 * jax.random.uniform(part_keys[3], (PAIRS,), jnp.float32) ** block_scale(part_keys[3], (PAIRS,), ((0, 8),), -0.2, 0.2), -1.5, -0.5),
        "col_energy": jnp.clip(0.5 + 2.5 * jax.random.uniform(part_keys[4], (NVP,), jnp.float32) ** block_scale(part_keys[4], (NVP,), ((0, 2),), -0.2, 0.2), 0.5, 3.0),
        "tile_irrep": place_ends(jax.random.randint(part_keys[5], (NVP // 128,), 0, IRREPS), jax.random.fold_in(part_keys[5], 1), 0, IRREPS - 1).astype(jnp.int32),
        "pair_irrep": draw_pair_irrep(jax.random.fold_in(jax.random.fold_in(key_of[8], part), 71), part),
        "mirror_slot": draw_mirror_slot(jax.random.fold_in(jax.random.fold_in(key_of[8], part), 71), part),
    }


def reference(amplitudes, driver, integrals, pair_energy, col_energy, tile_irrep, pair_irrep, mirror_slot):
    block_count = PAIRS // ROWS_DEV
    row_index = jnp.arange(PAIRS, dtype=jnp.int32)
    partner = (row_index // ROWS_DEV + block_count // 2) % block_count
    mirror = (partner * ROWS_DEV + mirror_slot).astype(jnp.int32)
    col_irrep = jnp.repeat(tile_irrep, 128)
    occupied = pair_irrep[:, None] == col_irrep[None, :]
    energy_gap = col_energy[None, :] - pair_energy[:, None]
    driver_wide = driver.astype(jnp.float32)
    current = jnp.where(occupied, amplitudes, jnp.zeros((), amplitudes.dtype))
    updated = driver_wide
    for iteration in range(ITERS):
        ladder = jnp.dot(current, integrals, preferred_element_type=jnp.float32)
        symmetric = ladder + ladder[mirror]
        updated = jnp.where(occupied, (driver_wide + symmetric) / energy_gap, jnp.zeros((), jnp.float32))
        current = updated.astype(jnp.bfloat16)
    return updated
```

```python
import functools

import jax
import jax.numpy as jnp
from jax import lax
from jax.experimental import pallas as pl
from jax.experimental.pallas import tpu as pltpu
from jax.sharding import PartitionSpec as P

ITERS = 2
TILE = 128
VMEM_BYTES = 48 * 1024 * 1024


def from_partner(value, axis, apart):
    return lax.ppermute(value, axis, [(i, i ^ 1 << apart) for i in range(lax.axis_size(axis))])


def contract(blocks, integrals):
    total = jnp.dot(
        blocks[0],
        lax.all_gather(integrals, "virt", axis=1, tiled=True),
        preferred_element_type=jnp.float32,
    )
    return lax.psum_scatter(total, "sub", scatter_dimension=1, tiled=True)


def dense_plan(
    amplitudes, driver, integrals, pair_energy, col_energy, tile_irrep, pair_irrep, mirror_slot
):
    col_irrep = jnp.repeat(tile_irrep, TILE)
    occupied = pair_irrep[:, None] == col_irrep[None, :]
    energy_gap = col_energy[None, :] - pair_energy[:, None]
    driver_wide = driver.astype(jnp.float32)
    partner_bit = lax.axis_size("pair").bit_length() - 2
    current = jnp.where(occupied, amplitudes, jnp.zeros((), amplitudes.dtype))
    updated = driver_wide
    for iteration in range(ITERS):
        ladder = contract((current,), integrals)
        mirror_block = from_partner(ladder, "pair", partner_bit)
        symmetric = ladder + jnp.take(mirror_block, mirror_slot, axis=0)
        updated = jnp.where(
            occupied, (driver_wide + symmetric) / energy_gap, jnp.zeros((), jnp.float32)
        )
        current = updated.astype(jnp.bfloat16)
    return updated


class Plan:
    def __init__(self, tiles, slab_tiles, places):
        self.tiles = tiles
        self.half = tiles // 2
        self.slab = slab_tiles
        self.places = places
        self.cap = 8 * slab_tiles
        self.shared = self.cap * 7 // 16
        self.direct = self.cap - 2 * self.shared


def label_of(own, other, sub, tile, half):
    place = lax.rem(tile, half)
    mine = (tile // half) == sub
    return jnp.where(mine, own[place], other[place])


def listed(plan, own, other, sub, slab, use):
    def step(i, count):
        j, k = i // plan.tiles, lax.rem(i, plan.tiles)
        here = label_of(own, other, sub, slab * plan.slab + j, plan.half)
        match = label_of(own, other, sub, k, plan.half) == here

        @pl.when(match & (count < plan.cap))
        def _():
            use(count, k, j)

        return count + match.astype(jnp.int32)

    return lax.fori_loop(0, plan.slab * plan.tiles, step, jnp.int32(0))


def tile_at(index):
    return pl.ds(pl.multiple_of(index * TILE, TILE), TILE)


def pack_kernel(plan, own, other, place, mine_ref, their_ref, shared_ref, direct_ref):
    slab, side, sub = place[0], place[1], place[2]

    def use(count, k, j):
        def copy(to_ref, slot):
            rows, cols = tile_at(lax.rem(k, plan.half)), tile_at(j)

            @pl.when((k // plan.half) == sub)
            def _():
                to_ref[tile_at(slot), :] = mine_ref[rows, cols]

            @pl.when((k // plan.half) != sub)
            def _():
                to_ref[tile_at(slot), :] = their_ref[rows, cols]

        slot = count - side * plan.shared

        @pl.when((slot >= 0) & (slot < plan.shared))
        def _():
            copy(shared_ref, slot)

        @pl.when(count >= 2 * plan.shared)
        def _():
            copy(direct_ref, count - 2 * plan.shared)

    shared_ref[...] = jnp.zeros_like(shared_ref)
    direct_ref[...] = jnp.zeros_like(direct_ref)
    listed(plan, own, other, sub, slab, use)


def update(rows, cols, sym, driver, gap_own, occupied):
    return jnp.where(occupied, (driver + sym) / gap_own, 0.0)


def first_kernel(plan, rounds, *refs):
    own, other, place, mine_ref, their_ref = refs[:5]
    parts = refs[5 : 5 + 3 * rounds]
    (cur_mine, cur_their, drv_own, drv_par, lab_row, pe_own, pe_par, col_energy) = refs[
        5 + 3 * rounds : 13 + 3 * rounds
    ]
    ints_ref, cur_ref = refs[13 + 3 * rounds :]
    z, side, sub = place[0], place[1], place[2]
    half_places = plan.places // 2
    width = plan.slab * TILE
    rows_half = plan.half * TILE
    ints_ref[...] = jnp.zeros_like(ints_ref)

    def fill(slab, rs, xs, us):
        first = (slab - sub * half_places) * plan.slab

        def use(count, k, j):
            rows, cols = tile_at(k), tile_at(first + j)

            def copy(from_ref, slot):
                ints_ref[rows, cols] = from_ref[tile_at(slot), :]

            in_first = count < plan.shared
            in_second = (count >= plan.shared) & (count < 2 * plan.shared)
            from_here = (in_first & (side == 0)) | (in_second & (side == 1))
            slot = jnp.where(in_first, count, count - plan.shared)

            @pl.when(from_here)
            def _():
                copy(rs, slot)

            @pl.when((in_first | in_second) & jnp.logical_not(from_here))
            def _():
                copy(xs, slot)

            @pl.when(count >= 2 * plan.shared)
            def _():
                copy(us, count - 2 * plan.shared)

        listed(plan, own, other, sub, slab, use)

    for r in range(1, rounds):
        slab = lax.rem(z - r + plan.places, plan.places)
        slab = jnp.where(
            slab // half_places == sub, slab, lax.rem(slab + half_places, plan.places)
        )
        fill(slab, *parts[3 * r : 3 * r + 3])

    @pl.when(z // half_places == sub)
    def _():
        cols = pl.ds(pl.multiple_of((z - sub * half_places) * width, TILE), width)
        mine_at = pl.ds(pl.multiple_of(sub * rows_half, TILE), rows_half)
        their_at = pl.ds(pl.multiple_of((1 - sub) * rows_half, TILE), rows_half)
        ints_ref[mine_at, cols] = mine_ref[...]
        ints_ref[their_at, cols] = their_ref[...]

    @pl.when(z // half_places != sub)
    def _():
        fill(lax.rem(z + half_places, plan.places), *parts[:3])

    multiply(
        plan, own, place, cur_mine, cur_their, ints_ref, drv_own, drv_par, lab_row, pe_own, pe_par,
        col_energy, cur_ref,
    )


def multiply(
    plan, own, place, cur_mine, cur_their, ints_ref, drv_own, drv_par, lab_row, pe_own, pe_par,
    col_energy, out_ref,
):
    sub = place[2]
    rows_half = plan.half * TILE
    mine_at = pl.ds(pl.multiple_of(sub * rows_half, TILE), rows_half)
    their_at = pl.ds(pl.multiple_of((1 - sub) * rows_half, TILE), rows_half)
    rows = drv_own.shape[0]
    wide = 2 * TILE

    def block(c, _):
        cols = pl.ds(pl.multiple_of(c * wide, wide), wide)
        total = jnp.dot(
            cur_mine[...], ints_ref[mine_at, cols], preferred_element_type=jnp.float32
        ) + jnp.dot(cur_their[...], ints_ref[their_at, cols], preferred_element_type=jnp.float32)
        sym = total[:rows] + total[rows:]
        for t in range(2):
            at = pl.ds(pl.multiple_of(c * wide + t * TILE, TILE), TILE)
            part = sym[:, t * TILE : (t + 1) * TILE]
            occupied = lab_row[...] == own[2 * c + t]
            energy = col_energy[:, at]
            new = jnp.where(
                occupied, (drv_own[:, at].astype(jnp.float32) + part) / (energy - pe_own[...]), 0.0
            )
            out_ref[:rows, at] = new.astype(out_ref.dtype)
            if out_ref.shape[0] > rows:
                new = jnp.where(
                    occupied,
                    (drv_par[:, at].astype(jnp.float32) + part) / (energy - pe_par[...]),
                    0.0,
                )
                out_ref[rows:, at] = new.astype(out_ref.dtype)
        return 0

    lax.fori_loop(0, plan.half // 2, block, 0)


def second_kernel(plan, own, place, cur_mine, cur_their, ints_ref, drv_own, lab_row, pe_own,
                  col_energy, out_ref):
    multiply(
        plan, own, place, cur_mine, cur_their, ints_ref, drv_own, None, lab_row, pe_own, None,
        col_energy, out_ref,
    )


def in_smem(count):
    return [pl.BlockSpec(memory_space=pltpu.SMEM)] * count


def in_vmem(count):
    return [pl.BlockSpec(memory_space=pltpu.VMEM)] * count


def call(kernel, smem, vmem, outs, flops=0):
    moved = sum(v.size * v.dtype.itemsize for v in vmem)
    single = not isinstance(outs, (list, tuple))
    return pl.pallas_call(
        kernel,
        out_shape=outs,
        in_specs=in_smem(len(smem)) + in_vmem(len(vmem)),
        out_specs=in_vmem(1)[0] if single else in_vmem(len(outs)),
        compiler_params=pltpu.CompilerParams(vmem_limit_bytes=VMEM_BYTES),
        cost_estimate=pl.CostEstimate(flops=flops, bytes_accessed=2 * moved, transcendentals=0),
    )(*smem, *vmem)


def body(
    amplitudes, driver, integrals, pair_energy, col_energy, tile_irrep, pair_irrep, mirror_slot
):
    places, sides = lax.axis_size("virt"), lax.axis_size("pair")
    partner_bit = sides.bit_length() - 2
    rows, half_cols = amplitudes.shape
    plan = Plan(2 * half_cols // TILE, integrals.shape[1] // TILE, places)
    half_places = places // 2
    z, sub = lax.axis_index("virt"), lax.axis_index("sub")
    side = (lax.axis_index("pair") >> partner_bit) & 1
    place = jnp.stack([z, side, sub]).astype(jnp.int32)

    other_irrep = from_partner(tile_irrep, "sub", 0)
    their_ints = from_partner(integrals, "sub", 0)

    occupied = pair_irrep[:, None] == jnp.repeat(tile_irrep, TILE)[None, :]
    masked = jnp.where(occupied, amplitudes, jnp.zeros((), amplitudes.dtype))
    mirror_amps = jnp.take(from_partner(masked, "pair", partner_bit), mirror_slot, axis=0)
    mirror_drv = jnp.take(from_partner(driver, "pair", partner_bit), mirror_slot, axis=0)
    mirror_energy = jnp.take(from_partner(pair_energy, "pair", partner_bit), mirror_slot, axis=0)
    cur_mine = jnp.concatenate([masked, mirror_amps], axis=0)
    cur_their = from_partner(cur_mine, "sub", 0)

    tile = jax.ShapeDtypeStruct((TILE, TILE), integrals.dtype)
    shared, direct = call(
        functools.partial(pack_kernel, plan),
        (tile_irrep, other_irrep, place),
        (integrals, their_ints),
        [
            jax.ShapeDtypeStruct((plan.shared * TILE, TILE), tile.dtype),
            jax.ShapeDtypeStruct((plan.direct * TILE, TILE), tile.dtype),
        ],
    )
    parts = []
    for r in range(half_places):
        pairs = []
        for i in range(places):
            for core in range(2):
                to = (i + r + half_places * (1 - core)) % places
                if to != i:
                    pairs.append((2 * i + core, 2 * to + i // half_places))
        got_shared = lax.ppermute(shared, ("virt", "sub"), pairs)
        got_direct = lax.ppermute(direct, ("virt", "sub"), pairs)
        parts += [got_shared, from_partner(got_shared, "pair", partner_bit), got_direct]

    lab_row = pair_irrep[:, None]
    pe_own, pe_par = pair_energy[:, None], mirror_energy[:, None]
    energy = col_energy[None, :]
    flops = 2 * 2 * rows * plan.tiles * TILE * half_cols
    ints, cur_mine = call(
        functools.partial(first_kernel, plan, half_places),
        (tile_irrep, other_irrep, place),
        (integrals, their_ints, *parts, cur_mine, cur_their, driver, mirror_drv, lab_row, pe_own,
         pe_par, energy),
        [
            jax.ShapeDtypeStruct((plan.tiles * TILE, half_cols), integrals.dtype),
            jax.ShapeDtypeStruct((2 * rows, half_cols), integrals.dtype),
        ],
        flops,
    )
    cur_their = from_partner(cur_mine, "sub", 0)

    def sparse_end():
        return call(
            functools.partial(second_kernel, plan),
            (tile_irrep, place),
            (cur_mine, cur_their, ints, driver, lab_row, pe_own, energy),
            jax.ShapeDtypeStruct((rows, half_cols), jnp.float32),
            flops,
        )

    def dense_end():
        return dense_plan(
            amplitudes, driver, integrals, pair_energy, col_energy, tile_irrep, pair_irrep,
            mirror_slot,
        )

    labels = jnp.concatenate([tile_irrep, other_irrep])
    by_slab = jnp.where(sub == 0, labels, jnp.roll(labels, plan.half))
    needed = (by_slab[:, None] == labels[None, :]).sum(axis=1).reshape(places, plan.slab).sum(axis=1)
    return lax.cond((needed > plan.cap).any(), dense_end, sparse_end)


def solution(mesh):
    return jax.shard_map(
        body,
        mesh=mesh,
        in_specs=(
            P(("groups", "pair", "virt"), "sub"),
            P(("groups", "pair", "virt"), "sub"),
            P(("groups", "sub"), "virt"),
            P(("groups", "pair", "virt")),
            P(("groups", "sub")),
            P(("groups", "sub")),
            P(("groups", "pair", "virt")),
            P(("groups", "pair", "virt")),
        ),
        out_specs=P(("groups", "pair", "virt"), "sub"),
        check_vma=False,
    )
```

```python
import functools

import jax
import jax.numpy as jnp
from jax import lax
from jax.experimental import pallas as pl
from jax.experimental.pallas import tpu as pltpu
from jax.sharding import PartitionSpec as P

ITERS = 2
TILE = 128
VMEM_BYTES = 48 * 1024 * 1024


def from_partner(value, axis, apart):
    return lax.ppermute(value, axis, [(i, i ^ 1 << apart) for i in range(lax.axis_size(axis))])


def contract(blocks, integrals):
    total = jnp.dot(
        blocks[0],
        lax.all_gather(integrals, "virt", axis=1, tiled=True),
        preferred_element_type=jnp.float32,
    )
    return lax.psum_scatter(total, "sub", scatter_dimension=1, tiled=True)


def dense_plan(
    amplitudes, driver, integrals, pair_energy, col_energy, tile_irrep, pair_irrep, mirror_slot
):
    col_irrep = jnp.repeat(tile_irrep, TILE)
    occupied = pair_irrep[:, None] == col_irrep[None, :]
    energy_gap = col_energy[None, :] - pair_energy[:, None]
    driver_wide = driver.astype(jnp.float32)
    partner_bit = lax.axis_size("pair").bit_length() - 2
    current = jnp.where(occupied, amplitudes, jnp.zeros((), amplitudes.dtype))
    updated = driver_wide
    for iteration in range(ITERS):
        ladder = contract((current,), integrals)
        mirror_block = from_partner(ladder, "pair", partner_bit)
        symmetric = ladder + jnp.take(mirror_block, mirror_slot, axis=0)
        updated = jnp.where(
            occupied, (driver_wide + symmetric) / energy_gap, jnp.zeros((), jnp.float32)
        )
        current = updated.astype(jnp.bfloat16)
    return updated


class Plan:
    def __init__(self, tiles, slab_tiles, places):
        self.tiles = tiles
        self.half = tiles // 2
        self.slab = slab_tiles
        self.places = places
        self.cap = 8 * slab_tiles
        self.shared = self.cap * 7 // 16
        self.direct = self.cap - 2 * self.shared


def tile_at(index):
    return pl.ds(pl.multiple_of(index * TILE, TILE), TILE)


def all_labels(plan, own, other, sub, labels):
    for i in range(plan.half):
        labels[sub * plan.half + i] = own[i]
        labels[(1 - sub) * plan.half + i] = other[i]


def list_tiles(plan, labels, slab, spots):
    for n in range(plan.cap):
        spots[n] = 0
    count = jnp.int32(0)
    for j in range(plan.slab):
        here = labels[slab * plan.slab + j]
        for k in range(plan.tiles):
            spots[count] = j * plan.tiles + k
            count += (labels[k] == here).astype(jnp.int32)
    for n in range(plan.cap):
        spots[n] = jnp.where(n < count, spots[n], 0)


def pack_kernel(
    plan, own, other, place, mine_ref, their_ref, shared_ref, direct_ref, full_ref, labels, spots,
    sizes,
):
    slab, side, sub = place[0], place[1], place[2]
    all_labels(plan, own, other, sub, labels)
    list_tiles(plan, labels, slab, spots)

    def copy(to_ref, first, count):
        def step(n, _):
            spot = spots[first + n]
            j, k = spot // plan.tiles, lax.rem(spot, plan.tiles)
            rows, cols = tile_at(lax.rem(k, plan.half)), tile_at(j)
            to_ref[tile_at(n), :] = jnp.where(
                k // plan.half == sub, mine_ref[rows, cols], their_ref[rows, cols]
            )
            return 0

        lax.fori_loop(0, count, step, 0)

    copy(shared_ref, side * plan.shared, plan.shared)
    copy(direct_ref, 2 * plan.shared, plan.direct)

    for k in range(plan.tiles):
        sizes[k] = 0
    for k in range(plan.tiles):
        sizes[labels[k]] += 1
    most = jnp.int32(0)
    for i in range(plan.places):
        needed = jnp.int32(0)
        for j in range(plan.slab):
            needed += sizes[labels[i * plan.slab + j]]
        most = jnp.maximum(most, needed)
    full_ref[0] = (most > plan.cap).astype(jnp.int32)


def column(row):
    n = row.shape[1]
    here = lax.broadcasted_iota(jnp.int32, (n, n), 0) == lax.broadcasted_iota(jnp.int32, (n, n), 1)
    return jnp.sum(jnp.where(here, row.astype(jnp.float32), 0.0), axis=1, keepdims=True)


def mirror_table(slot_row):
    n = slot_row.shape[1]
    slots = column(slot_row).astype(jnp.int32)
    return lax.broadcasted_iota(jnp.int32, (n, n), 1) == slots


def mirror_kernel(plan, own, amps_ref, other_amps_ref, label_row, slot_row, after_ref, cur_ref):
    rows = amps_ref.shape[0]
    table = mirror_table(slot_row[...]).astype(jnp.bfloat16)
    row_label = column(label_row[...]).astype(jnp.int32)
    zero = jnp.zeros((), cur_ref.dtype)
    for j in range(plan.half):
        cols = slice(j * TILE, (j + 1) * TILE)
        occupied = row_label == own[j]
        cur_ref[:rows, cols] = jnp.where(occupied, amps_ref[:, cols], zero)
        mirrored = jnp.dot(table, other_amps_ref[:, cols], preferred_element_type=jnp.float32)
        cur_ref[rows:, cols] = jnp.where(occupied, mirrored, 0.0).astype(cur_ref.dtype)


def multiply(plan, own, place, cur_mine, cur_their, ints_ref, row_label, energies, drivers,
             col_energy, out_ref):
    sub = place[2]
    rows_half = plan.half * TILE
    mine_at = pl.ds(pl.multiple_of(sub * rows_half, TILE), rows_half)
    their_at = pl.ds(pl.multiple_of((1 - sub) * rows_half, TILE), rows_half)
    rows = row_label.shape[0]
    wide = 2 * TILE

    def block(c, _):
        cols = pl.ds(pl.multiple_of(c * wide, wide), wide)
        total = jnp.dot(
            cur_mine[...], ints_ref[mine_at, cols], preferred_element_type=jnp.float32
        ) + jnp.dot(cur_their[...], ints_ref[their_at, cols], preferred_element_type=jnp.float32)
        sym = total[:rows] + total[rows:]
        for t in range(2):
            at = pl.ds(pl.multiple_of(c * wide + t * TILE, TILE), TILE)
            part = sym[:, t * TILE : (t + 1) * TILE]
            occupied = row_label == own[2 * c + t]
            energy = col_energy[:, at]
            for i, (pair_energy, driver) in enumerate(zip(energies, drivers)):
                new = (driver[:, at].astype(jnp.float32) + part) / (energy - pair_energy)
                new = jnp.where(occupied, new, 0.0)
                out_ref[i * rows : (i + 1) * rows, at] = new.astype(out_ref.dtype)
        return 0

    lax.fori_loop(0, plan.half // 2, block, 0)


def first_kernel(plan, rounds, *refs):
    own, other, place, mine_ref, their_ref = refs[:5]
    parts = refs[5 : 5 + 3 * rounds]
    (cur_mine, cur_their, driver, other_driver, label_row, slot_row, energy_row, other_energy_row,
     col_energy) = refs[5 + 3 * rounds : 14 + 3 * rounds]
    ints_ref, cur_ref, mirror_driver, labels, spots = refs[14 + 3 * rounds :]
    z, side, sub = place[0], place[1], place[2]
    half_places = plan.places // 2
    width = plan.slab * TILE
    rows_half = plan.half * TILE
    ints_ref[...] = jnp.zeros_like(ints_ref)
    all_labels(plan, own, other, sub, labels)

    def fill(slab, rs, xs, us):
        first = (slab - sub * half_places) * plan.slab
        list_tiles(plan, labels, slab, spots)

        def put(n, value):
            spot = spots[n]
            j, k = spot // plan.tiles, lax.rem(spot, plan.tiles)
            ints_ref[tile_at(k), tile_at(first + j)] = value

        def step(n, _):
            a, b = rs[tile_at(n), :], xs[tile_at(n), :]
            put(n, jnp.where(side == 0, a, b))
            put(plan.shared + n, jnp.where(side == 0, b, a))
            return 0

        lax.fori_loop(0, plan.shared, step, 0)

        def step_direct(n, _):
            put(2 * plan.shared + n, us[tile_at(n), :])
            return 0

        lax.fori_loop(0, plan.direct, step_direct, 0)

    for r in range(1, rounds):
        slab = lax.rem(z - r + plan.places, plan.places)
        slab = jnp.where(
            slab // half_places == sub, slab, lax.rem(slab + half_places, plan.places)
        )
        fill(slab, *parts[3 * r : 3 * r + 3])

    @pl.when(z // half_places == sub)
    def _():
        cols = pl.ds(pl.multiple_of((z - sub * half_places) * width, TILE), width)
        mine_at = pl.ds(pl.multiple_of(sub * rows_half, TILE), rows_half)
        their_at = pl.ds(pl.multiple_of((1 - sub) * rows_half, TILE), rows_half)
        ints_ref[mine_at, cols] = mine_ref[...]
        ints_ref[their_at, cols] = their_ref[...]

    @pl.when(z // half_places != sub)
    def _():
        fill(lax.rem(z + half_places, plan.places), *parts[:3])

    table = mirror_table(slot_row[...])
    mirror_driver[...] = jnp.dot(
        table.astype(jnp.bfloat16), other_driver[...], preferred_element_type=jnp.float32
    ).astype(mirror_driver.dtype)
    mirror_energy = jnp.sum(jnp.where(table, other_energy_row[...], 0.0), axis=1, keepdims=True)
    multiply(
        plan, own, place, cur_mine, cur_their, ints_ref, column(label_row[...]).astype(jnp.int32),
        (column(energy_row[...]), mirror_energy), (driver, mirror_driver), col_energy, cur_ref,
    )


def second_kernel(plan, own, place, cur_mine, cur_their, ints_ref, driver, label_row, energy_row,
                  col_energy, out_ref):
    multiply(
        plan, own, place, cur_mine, cur_their, ints_ref, column(label_row[...]).astype(jnp.int32),
        (column(energy_row[...]),), (driver,), col_energy, out_ref,
    )


def call(kernel, smem, vmem, outs, scratch=(), anywhere=(), flag=False, flops=0):
    moved = sum(v.size * v.dtype.itemsize for v in vmem)
    in_smem, in_vmem = pl.BlockSpec(memory_space=pltpu.SMEM), pl.BlockSpec(memory_space=pltpu.VMEM)
    in_any = pl.BlockSpec(memory_space=pl.ANY)
    return pl.pallas_call(
        kernel,
        out_shape=list(outs) + [jax.ShapeDtypeStruct((1,), jnp.int32)] * flag,
        in_specs=[in_smem] * len(smem) + [in_vmem] * len(vmem) + [in_any] * len(anywhere),
        out_specs=[in_vmem] * len(outs) + [in_smem] * flag,
        scratch_shapes=scratch,
        compiler_params=pltpu.CompilerParams(vmem_limit_bytes=VMEM_BYTES),
        cost_estimate=pl.CostEstimate(flops=flops, bytes_accessed=2 * moved, transcendentals=0),
    )(*smem, *vmem, *anywhere)


def body(
    amplitudes, driver, integrals, pair_energy, col_energy, tile_irrep, pair_irrep, mirror_slot
):
    places, sides = lax.axis_size("virt"), lax.axis_size("pair")
    partner_bit = sides.bit_length() - 2
    rows, half_cols = amplitudes.shape
    plan = Plan(2 * half_cols // TILE, integrals.shape[1] // TILE, places)
    half_places = places // 2
    z, sub = lax.axis_index("virt"), lax.axis_index("sub")
    side = (lax.axis_index("pair") >> partner_bit) & 1
    place = jnp.stack([z, side, sub]).astype(jnp.int32)

    def like(shape, dtype=integrals.dtype):
        return jax.ShapeDtypeStruct(shape, dtype)

    other_irrep = from_partner(tile_irrep, "sub", 0)
    their_ints = from_partner(integrals, "sub", 0)
    other_amps = from_partner(amplitudes, "pair", partner_bit)
    other_driver = from_partner(driver, "pair", partner_bit)
    other_energy = from_partner(pair_energy, "pair", partner_bit)

    lists = [pltpu.SMEM((plan.tiles,), jnp.int32), pltpu.SMEM((plan.slab * plan.tiles + 1,), jnp.int32)]
    shared, direct, full = call(
        functools.partial(pack_kernel, plan),
        (tile_irrep, other_irrep, place),
        (integrals, their_ints),
        [like((plan.shared * TILE, TILE)), like((plan.direct * TILE, TILE))],
        lists + [pltpu.SMEM((plan.tiles,), jnp.int32)],
        flag=True,
    )
    groups = lax.axis_size("groups")
    ends = full
    for apart in range(1, groups):
        ends = jnp.maximum(
            ends, lax.ppermute(full, "groups", [(i, (i + apart) % groups) for i in range(groups)])
        )
    parts = []
    for r in range(half_places):
        pairs = []
        for i in range(places):
            for core in range(2):
                to = (i + r + half_places * (1 - core)) % places
                if to != i:
                    pairs.append((2 * i + core, 2 * to + i // half_places))
        got_shared = lax.ppermute(shared, ("virt", "sub"), pairs)
        got_direct = lax.ppermute(direct, ("virt", "sub"), pairs)
        parts += [got_shared, from_partner(got_shared, "pair", partner_bit), got_direct]

    label_row, slot_row = pair_irrep[None, :], mirror_slot[None, :]
    (cur_mine,) = call(
        functools.partial(mirror_kernel, plan),
        (tile_irrep,),
        (amplitudes, other_amps, label_row, slot_row),
        [like((2 * rows, half_cols))],
        anywhere=(direct,),
    )
    cur_their = from_partner(cur_mine, "sub", 0)

    energy_row, energy = pair_energy[None, :], col_energy[None, :]
    flops = 2 * 2 * rows * plan.tiles * TILE * half_cols
    ints, cur_mine = call(
        functools.partial(first_kernel, plan, half_places),
        (tile_irrep, other_irrep, place),
        (integrals, their_ints, *parts, cur_mine, cur_their, driver, other_driver, label_row,
         slot_row, energy_row, other_energy[None, :], energy),
        [like((plan.tiles * TILE, half_cols)), like((2 * rows, half_cols))],
        [pltpu.VMEM((rows, half_cols), driver.dtype)] + lists,
        flops=flops,
    )
    cur_their = from_partner(cur_mine, "sub", 0)

    def sparse_end():
        return call(
            functools.partial(second_kernel, plan),
            (tile_irrep, place),
            (cur_mine, cur_their, ints, driver, label_row, energy_row, energy),
            [like((rows, half_cols), jnp.float32)],
            flops=flops,
        )[0]

    def dense_end():
        return dense_plan(
            amplitudes, driver, integrals, pair_energy, col_energy, tile_irrep, pair_irrep,
            mirror_slot,
        )

    return lax.cond(ends[0] > 0, dense_end, sparse_end)


def solution(mesh):
    return jax.shard_map(
        body,
        mesh=mesh,
        in_specs=(
            P(("groups", "pair", "virt"), "sub"),
            P(("groups", "pair", "virt"), "sub"),
            P(("groups", "sub"), "virt"),
            P(("groups", "pair", "virt")),
            P(("groups", "sub")),
            P(("groups", "sub")),
            P(("groups", "pair", "virt")),
            P(("groups", "pair", "virt")),
        ),
        out_specs=P(("groups", "pair", "virt"), "sub"),
        check_vma=False,
    )
```

```python
import functools

import jax
import jax.numpy as jnp
from jax import lax
from jax.experimental import pallas as pl
from jax.experimental.pallas import tpu as pltpu
from jax.sharding import PartitionSpec as P

ITERS = 2
TILE = 128
VMEM_BYTES = 48 * 1024 * 1024


def from_partner(value, axis, apart):
    return lax.ppermute(value, axis, [(i, i ^ 1 << apart) for i in range(lax.axis_size(axis))])


def contract(blocks, integrals):
    places, z, sub = lax.axis_size("virt"), lax.axis_index("virt"), lax.axis_index("sub")
    width = integrals.shape[1]
    whole = jnp.zeros((integrals.shape[0], places * width), integrals.dtype)
    for apart in range(places):
        slab = integrals
        if apart:
            slab = lax.ppermute(
                integrals, "virt", [(i, (i + apart) % places) for i in range(places)]
            )
        at = lax.rem(z - apart + places, places) * width
        whole = lax.dynamic_update_slice(whole, slab, (0, at))
    total = jnp.dot(blocks[0], whole, preferred_element_type=jnp.float32)
    half = total.shape[1] // 2
    mine = lax.dynamic_slice_in_dim(total, sub * half, half, 1)
    theirs = lax.dynamic_slice_in_dim(total, (1 - sub) * half, half, 1)
    return mine + from_partner(theirs, "sub", 0)


def dense_plan(
    amplitudes, driver, integrals, pair_energy, col_energy, tile_irrep, pair_irrep, mirror_slot
):
    col_irrep = jnp.repeat(tile_irrep, TILE)
    occupied = pair_irrep[:, None] == col_irrep[None, :]
    energy_gap = col_energy[None, :] - pair_energy[:, None]
    driver_wide = driver.astype(jnp.float32)
    partner_bit = lax.axis_size("pair").bit_length() - 2
    current = jnp.where(occupied, amplitudes, jnp.zeros((), amplitudes.dtype))
    updated = driver_wide
    for iteration in range(ITERS):
        ladder = contract((current,), integrals)
        mirror_block = from_partner(ladder, "pair", partner_bit)
        symmetric = ladder + jnp.take(mirror_block, mirror_slot, axis=0)
        updated = jnp.where(
            occupied, (driver_wide + symmetric) / energy_gap, jnp.zeros((), jnp.float32)
        )
        current = updated.astype(jnp.bfloat16)
    return updated


class Plan:
    def __init__(self, tiles, slab_tiles, places):
        self.tiles = tiles
        self.half = tiles // 2
        self.slab = slab_tiles
        self.places = places
        self.near = places // 2
        self.cap = 8 * slab_tiles
        self.part = self.cap // 2


def tile_at(index):
    return pl.ds(pl.multiple_of(index * TILE, TILE), TILE)


def all_labels(plan, own, other, sub, labels):
    for i in range(plan.half):
        labels[sub * plan.half + i] = own[i]
        labels[(1 - sub) * plan.half + i] = other[i]


def list_tiles(plan, labels, slab, spots):
    for n in range(plan.cap):
        spots[n] = 0
    count = jnp.int32(0)
    for j in range(plan.slab):
        here = labels[slab * plan.slab + j]
        for k in range(plan.tiles):
            spots[count] = j * plan.tiles + k
            count += (labels[k] == here).astype(jnp.int32)
    for n in range(plan.cap):
        spots[n] = jnp.where(n < count, spots[n], 0)


def pack_kernel(
    plan, own, other, place, mine_ref, their_ref, amps_ref, label_row, energy_row, send0_ref,
    send1_ref, masked_ref, full_ref, labels, spots, sizes,
):
    slab, side, sub = place[0], place[1], place[2]
    all_labels(plan, own, other, sub, labels)
    list_tiles(plan, labels, slab, spots)
    is_near = slab // plan.near == sub

    for i, to_ref in enumerate((send0_ref, send1_ref)):
        first = jnp.where(is_near, i, side) * plan.part

        def step(n, _):
            spot = spots[first + n]
            j, k = spot // plan.tiles, lax.rem(spot, plan.tiles)
            rows, cols = tile_at(lax.rem(k, plan.half)), tile_at(j)
            to_ref[tile_at(n), :] = jnp.where(
                k // plan.half == sub, mine_ref[rows, cols], their_ref[rows, cols]
            )
            return 0

        lax.fori_loop(0, plan.part, step, 0)

    rows = amps_ref.shape[0]
    row_label = column(label_row[...]).astype(jnp.int32)
    for j in range(plan.half):
        cols = slice(j * TILE, (j + 1) * TILE)
        amps = amps_ref[:, cols]
        masked_ref[:rows, cols] = jnp.where(row_label == own[j], amps, jnp.zeros((), amps.dtype))

    masked_ref[rows:, :] = jnp.zeros_like(masked_ref[rows:, :])
    rest = jnp.broadcast_to(energy_row[...], (16, rows))
    at = lax.broadcasted_iota(jnp.int32, (16, rows), 0)
    terms = jnp.zeros((16, rows), jnp.float32)
    for i in range(3):
        term = rest.astype(jnp.bfloat16).astype(jnp.float32)
        terms = jnp.where(at == i, term, terms)
        rest = rest - term
    masked_ref[rows:, :rows] = terms.astype(jnp.bfloat16)

    for k in range(plan.tiles):
        sizes[k] = 0
    for k in range(plan.tiles):
        sizes[labels[k]] += 1
    most = jnp.int32(0)
    for i in range(plan.places):
        needed = jnp.int32(0)
        for j in range(plan.slab):
            needed += sizes[labels[i * plan.slab + j]]
        most = jnp.maximum(most, needed)
    full_ref[0] = (most > plan.cap).astype(jnp.int32)


def column(row):
    n = row.shape[1]
    here = lax.broadcasted_iota(jnp.int32, (n, n), 0) == lax.broadcasted_iota(jnp.int32, (n, n), 1)
    return jnp.sum(jnp.where(here, row.astype(jnp.float32), 0.0), axis=1, keepdims=True)


def mirror_table(slot_row):
    n = slot_row.shape[1]
    slots = column(slot_row).astype(jnp.int32)
    return lax.broadcasted_iota(jnp.int32, (n, n), 1) == slots


def mirror_kernel(
    masked_ref, other_masked_ref, other_driver_ref, slot_row, label_row, energy_row, after_ref,
    cur_ref, mirror_driver_ref, columns_ref,
):
    rows = mirror_driver_ref.shape[0]
    table = mirror_table(slot_row[...])
    weights = table.astype(jnp.bfloat16)
    cur_ref[:rows, :] = masked_ref[:rows, :]
    cur_ref[rows:, :] = jnp.dot(
        weights, other_masked_ref[:rows, :], preferred_element_type=jnp.float32
    ).astype(cur_ref.dtype)
    mirror_driver_ref[...] = jnp.dot(
        weights, other_driver_ref[...], preferred_element_type=jnp.float32
    ).astype(mirror_driver_ref.dtype)
    terms = other_masked_ref[rows:, :rows].astype(jnp.float32)
    other_energy = (terms[0:1] + terms[1:2]) + terms[2:3]
    mirror_energy = jnp.sum(jnp.where(table, other_energy, 0.0), axis=1, keepdims=True)
    for i, value in enumerate((column(label_row[...]), column(energy_row[...]), mirror_energy)):
        columns_ref[i * rows : (i + 1) * rows, :] = jnp.broadcast_to(value, (rows, TILE))


def halves(plan, sub):
    rows = plan.half * TILE
    return (
        pl.ds(pl.multiple_of(sub * rows, TILE), rows),
        pl.ds(pl.multiple_of((1 - sub) * rows, TILE), rows),
    )


WIDE = 2 * TILE


def first_kernel(plan, rounds, *refs):
    own, other, place, ends, mine_ref, their_ref, cur_mine, cur_their, driver, mirror_driver = refs[:10]
    columns, col_energy = refs[10:12]
    got = refs[12 : 12 + rounds]
    swapped = refs[12 + rounds : 12 + rounds + plan.near]
    ints_ref, cur_ref, end_ref, labels, spots = refs[12 + rounds + plan.near :]
    z, side, sub = place[0], place[1], place[2]
    width = plan.slab * TILE
    mine_at, their_at = halves(plan, sub)
    end_ref[0] = ends[0]
    ints_ref[...] = jnp.zeros_like(ints_ref)
    all_labels(plan, own, other, sub, labels)
    here = lax.rem(z, plan.near)

    def fill(place, low_ref, high_ref, turn):
        list_tiles(plan, labels, sub * plan.near + place, spots)

        def put(n, value):
            spot = spots[n]
            j, k = spot // plan.tiles, lax.rem(spot, plan.tiles)
            ints_ref[tile_at(k), tile_at(place * plan.slab + j)] = value

        def step(n, _):
            low, high = low_ref[tile_at(n), :], high_ref[tile_at(n), :]
            put(n, jnp.where(turn, high, low))
            put(plan.part + n, jnp.where(turn, low, high))
            return 0

        lax.fori_loop(0, plan.part, step, 0)

    @pl.when(z // plan.near == sub)
    def _():
        cols = pl.ds(pl.multiple_of(here * width, TILE), width)
        ints_ref[mine_at, cols] = mine_ref[...]
        ints_ref[their_at, cols] = their_ref[...]
        for r in range(1, plan.near):
            fill(lax.rem(here + plan.near - r, plan.near), got[2 * r - 2], got[2 * r - 1], False)

    @pl.when(z // plan.near != sub)
    def _():
        for r in range(plan.near):
            fill(lax.rem(here + plan.near - r, plan.near), got[r], swapped[r], side == 1)

    rows = driver.shape[0]

    def block(c, _):
        cols = pl.ds(pl.multiple_of(c * WIDE, WIDE), WIDE)
        total = jnp.dot(
            cur_mine[...], ints_ref[mine_at, cols], preferred_element_type=jnp.float32
        ) + jnp.dot(cur_their[...], ints_ref[their_at, cols], preferred_element_type=jnp.float32)
        sym = total[:rows] + total[rows:]
        for t in range(2):
            at = pl.ds(pl.multiple_of(c * WIDE + t * TILE, TILE), TILE)
            part = sym[:, t * TILE : (t + 1) * TILE]
            occupied = columns[:rows] == own[2 * c + t].astype(jnp.float32)
            for i, source in enumerate((driver, mirror_driver)):
                gap = col_energy[:, at] - columns[(i + 1) * rows : (i + 2) * rows]
                new = (source[:, at].astype(jnp.float32) + part) / gap
                new = jnp.where(occupied, new, 0.0)
                cur_ref[i * rows : (i + 1) * rows, at] = new.astype(cur_ref.dtype)
        return 0

    lax.fori_loop(0, plan.half // 2, block, 0)


def part_kernel(plan, place, cur_ref, ints_ref, sym_ref):
    mine_at, _ = halves(plan, place[2])
    rows = sym_ref.shape[0]

    def block(c, _):
        cols = pl.ds(pl.multiple_of(c * WIDE, WIDE), WIDE)
        total = jnp.dot(cur_ref[...], ints_ref[mine_at, cols], preferred_element_type=jnp.float32)
        sym_ref[:, cols] = total[:rows] + total[rows:]
        return 0

    lax.fori_loop(0, plan.half // 2, block, 0)


def last_kernel(
    plan, own, place, cur_ref, ints_ref, sym_ref, driver, columns, col_energy, out_ref, new_ref, sems
):
    _, their_at = halves(plan, place[2])
    rows = driver.shape[0]
    copies = []
    for c in range(plan.half // 2):
        cols = slice(c * WIDE, (c + 1) * WIDE)
        total = jnp.dot(cur_ref[...], ints_ref[their_at, cols], preferred_element_type=jnp.float32)
        sym = sym_ref[:, cols] + (total[:rows] + total[rows:])
        for t in range(2):
            at = slice(c * WIDE + t * TILE, c * WIDE + (t + 1) * TILE)
            occupied = columns[:rows] == own[2 * c + t].astype(jnp.float32)
            gap = col_energy[:, at] - columns[rows : 2 * rows]
            new = (driver[:, at].astype(jnp.float32) + sym[:, t * TILE : (t + 1) * TILE]) / gap
            new_ref[:, at] = jnp.where(occupied, new, 0.0)
        copy = pltpu.make_async_copy(new_ref.at[:, cols], out_ref.at[:, cols], sems.at[c])
        copy.start()
        copies.append(copy)
    for copy in copies:
        copy.wait()


def call(kernel, smem, vmem, outs, scratch=(), anywhere=(), flag=False, flops=0, to_any=False):
    moved = sum(v.size * v.dtype.itemsize for v in vmem)
    in_smem, in_vmem = pl.BlockSpec(memory_space=pltpu.SMEM), pl.BlockSpec(memory_space=pltpu.VMEM)
    in_any = pl.BlockSpec(memory_space=pl.ANY)
    return pl.pallas_call(
        kernel,
        out_shape=list(outs) + [jax.ShapeDtypeStruct((1,), jnp.int32)] * flag,
        in_specs=[in_smem] * len(smem) + [in_vmem] * len(vmem) + [in_any] * len(anywhere),
        out_specs=[in_any if to_any else in_vmem] * len(outs) + [in_smem] * flag,
        scratch_shapes=scratch,
        compiler_params=pltpu.CompilerParams(vmem_limit_bytes=VMEM_BYTES),
        cost_estimate=pl.CostEstimate(flops=flops, bytes_accessed=2 * moved, transcendentals=0),
    )(*smem, *vmem, *anywhere)


def body(
    amplitudes, driver, integrals, pair_energy, col_energy, tile_irrep, pair_irrep, mirror_slot
):
    places, sides = lax.axis_size("virt"), lax.axis_size("pair")
    partner_bit = sides.bit_length() - 2
    rows, half_cols = amplitudes.shape
    plan = Plan(2 * half_cols // TILE, integrals.shape[1] // TILE, places)
    z, sub = lax.axis_index("virt"), lax.axis_index("sub")
    side = (lax.axis_index("pair") >> partner_bit) & 1
    place = jnp.stack([z, side, sub]).astype(jnp.int32)

    def like(shape, dtype=integrals.dtype):
        return jax.ShapeDtypeStruct(shape, dtype)

    def over_pair(value):
        return from_partner(value, "pair", partner_bit)

    other_irrep = from_partner(tile_irrep, "sub", 0)
    their_ints = from_partner(integrals, "sub", 0)
    other_driver = over_pair(driver)

    label_row, slot_row, energy_row = pair_irrep[None, :], mirror_slot[None, :], pair_energy[None, :]
    lists = [pltpu.SMEM((plan.tiles,), jnp.int32), pltpu.SMEM((plan.slab * plan.tiles + 1,), jnp.int32)]
    *sends, masked, full = call(
        functools.partial(pack_kernel, plan),
        (tile_irrep, other_irrep, place),
        (integrals, their_ints, amplitudes, label_row, energy_row),
        [like((plan.part * TILE, TILE))] * 2 + [like((rows + 16, half_cols))],
        lists + [pltpu.SMEM((plan.tiles,), jnp.int32)],
        flag=True,
    )

    near = plan.near
    got = []
    for turn in range(max(2 * (near - 1), near)):
        pairs = []
        for i in range(places):
            half, at = i // near, i % near
            if turn < 2 * (near - 1):
                to = half * near + (at + turn // 2 + 1) % near
                pairs.append((2 * i + half, 2 * to + half))
            if turn < near:
                to = (1 - half) * near + (at + turn) % near
                pairs.append((2 * i + 1 - half, 2 * to + half))
        got.append(lax.ppermute(sends[turn % 2], ("virt", "sub"), pairs))
    pairs = []
    for i in range(places):
        for j in range(sides):
            far = 1 - i // near
            pairs.append(((i * sides + j) * 2 + far, (i * sides + (j ^ 1 << partner_bit)) * 2 + far))
    swapped = [lax.ppermute(value, ("virt", "pair", "sub"), pairs) for value in got[:near]]

    groups = lax.axis_size("groups")
    ends = full
    for apart in range(1, groups):
        ends = jnp.maximum(
            ends, lax.ppermute(full, "groups", [(i, (i + apart) % groups) for i in range(groups)])
        )

    cur_mine, mirror_driver, columns = call(
        mirror_kernel,
        (),
        (masked, over_pair(masked), other_driver, slot_row, label_row, energy_row),
        [like((2 * rows, half_cols)), like((rows, half_cols)), like((3 * rows, TILE), jnp.float32)],
        anywhere=(got[0],),
    )
    cur_their = from_partner(cur_mine, "sub", 0)

    energy = col_energy[None, :]
    flops = 2 * 2 * rows * plan.tiles * TILE * half_cols
    ints, cur_mine, ends = call(
        functools.partial(first_kernel, plan, len(got)),
        (tile_irrep, other_irrep, place, ends),
        (integrals, their_ints, cur_mine, cur_their, driver, mirror_driver, columns, energy, *got,
         *swapped),
        [like((plan.tiles * TILE, half_cols)), like((2 * rows, half_cols))],
        lists,
        flag=True,
        flops=flops,
    )
    cur_their = from_partner(cur_mine, "sub", 0)
    (sym,) = call(
        functools.partial(part_kernel, plan),
        (place,),
        (cur_mine, ints),
        [like((rows, half_cols), jnp.float32)],
        flops=flops // 2,
    )

    def sparse_end():
        return call(
            functools.partial(last_kernel, plan),
            (tile_irrep, place),
            (cur_their, ints, sym, driver, columns, energy),
            [like((rows, half_cols), jnp.float32)],
            [pltpu.VMEM((rows, half_cols), jnp.float32),
             pltpu.SemaphoreType.DMA((plan.half // 2,))],
            flops=flops // 2,
            to_any=True,
        )[0]

    def dense_end():
        return dense_plan(
            amplitudes, driver, integrals, pair_energy, col_energy, tile_irrep, pair_irrep,
            mirror_slot,
        )

    return lax.cond(ends[0] > 0, dense_end, sparse_end)


def solution(mesh):
    return jax.shard_map(
        body,
        mesh=mesh,
        in_specs=(
            P(("groups", "pair", "virt"), "sub"),
            P(("groups", "pair", "virt"), "sub"),
            P(("groups", "sub"), "virt"),
            P(("groups", "pair", "virt")),
            P(("groups", "sub")),
            P(("groups", "sub")),
            P(("groups", "pair", "virt")),
            P(("groups", "pair", "virt")),
        ),
        out_specs=P(("groups", "pair", "virt"), "sub"),
        check_vma=False,
    )
```

```python
import functools

import jax
import jax.numpy as jnp
from jax import lax
from jax.experimental import pallas as pl
from jax.experimental.pallas import tpu as pltpu
from jax.sharding import PartitionSpec as P

ITERS = 2
TILE = 128
IRREPS = 4
PIECES = 2
CHUNK = 16
CAPS = (5, 6, 7, 8)
VMEM_BYTES = 20 * 1024 * 1024


def from_partner(value, axis, apart):
    return lax.ppermute(value, axis, [(i, i ^ 1 << apart) for i in range(lax.axis_size(axis))])


def contract(blocks, integrals):
    places, z, sub = lax.axis_size("virt"), lax.axis_index("virt"), lax.axis_index("sub")
    width = integrals.shape[1]
    whole = jnp.zeros((integrals.shape[0], places * width), integrals.dtype)
    for apart in range(places):
        slab = integrals
        if apart:
            slab = lax.ppermute(
                integrals, "virt", [(i, (i + apart) % places) for i in range(places)]
            )
        at = lax.rem(z - apart + places, places) * width
        whole = lax.dynamic_update_slice(whole, slab, (0, at))
    total = jnp.dot(blocks[0], whole, preferred_element_type=jnp.float32)
    half = total.shape[1] // 2
    mine = lax.dynamic_slice_in_dim(total, sub * half, half, 1)
    theirs = lax.dynamic_slice_in_dim(total, (1 - sub) * half, half, 1)
    return mine + from_partner(theirs, "sub", 0)


def dense_plan(
    amplitudes, driver, integrals, pair_energy, col_energy, tile_irrep, pair_irrep, mirror_slot
):
    col_irrep = jnp.repeat(tile_irrep, TILE)
    occupied = pair_irrep[:, None] == col_irrep[None, :]
    energy_gap = col_energy[None, :] - pair_energy[:, None]
    driver_wide = driver.astype(jnp.float32)
    partner_bit = lax.axis_size("pair").bit_length() - 2
    current = jnp.where(occupied, amplitudes, jnp.zeros((), amplitudes.dtype))
    updated = driver_wide
    for iteration in range(ITERS):
        ladder = contract((current,), integrals)
        mirror_block = from_partner(ladder, "pair", partner_bit)
        symmetric = ladder + jnp.take(mirror_block, mirror_slot, axis=0)
        updated = jnp.where(
            occupied, (driver_wide + symmetric) / energy_gap, jnp.zeros((), jnp.float32)
        )
        current = updated.astype(jnp.bfloat16)
    return updated


class Plan:
    def __init__(self, tiles, slab_tiles, places, cap):
        self.tiles = tiles
        self.half = tiles // 2
        self.slab = slab_tiles
        self.places = places
        self.near = places // 2
        self.cap = cap
        self.part = self.cap // 2


def tile_at(index):
    return pl.ds(pl.multiple_of(index * TILE, TILE), TILE)


def all_labels(plan, own, other, sub, labels):
    for i in range(plan.half):
        labels[sub * plan.half + i] = own[i]
        labels[(1 - sub) * plan.half + i] = other[i]


def list_tiles(plan, labels, slab, spots):
    for n in range(plan.cap):
        spots[n] = 0
    count = jnp.int32(0)
    for j in range(plan.slab):
        here = labels[slab * plan.slab + j]
        for k in range(plan.tiles):
            spots[count] = j * plan.tiles + k
            count += (labels[k] == here).astype(jnp.int32)
    for n in range(plan.cap):
        spots[n] = jnp.where(n < count, spots[n], 0)


def pack_kernel(plans, own, other, place, mine_ref, their_ref, after_ref, *refs):
    *send_refs, level_ref, labels, spots, sizes = refs
    plan = plans[-1]
    slab, side, sub = place[0], place[1], place[2]
    all_labels(plan, own, other, sub, labels)

    for k in range(plan.tiles):
        sizes[k] = 0
    for k in range(plan.tiles):
        sizes[labels[k]] += 1
    most = jnp.int32(0)
    for i in range(plan.places):
        needed = jnp.int32(0)
        for j in range(plan.slab):
            needed += sizes[labels[i * plan.slab + j]]
        most = jnp.maximum(most, needed)
    level = jnp.int32(0)
    for each in plans:
        level += (most > each.cap).astype(jnp.int32)
    level_ref[0] = level

    list_tiles(plan, labels, slab, spots)
    is_near = slab // plan.near == sub
    for index, each in enumerate(plans):

        @pl.when(level == index)
        def _():
            for i in range(2):
                to_ref = send_refs[2 * index + i]
                first = jnp.where(is_near, i, side) * each.part
                for n in range(each.part):
                    spot = spots[first + n]
                    j, k = spot // plan.tiles, lax.rem(spot, plan.tiles)
                    rows, cols = tile_at(lax.rem(k, plan.half)), tile_at(j)
                    to_ref[n * TILE : (n + 1) * TILE, :] = jnp.where(
                        k // plan.half == sub, mine_ref[rows, cols], their_ref[rows, cols]
                    )


def column(row):
    n = row.shape[1]
    here = lax.broadcasted_iota(jnp.int32, (n, n), 0) == lax.broadcasted_iota(jnp.int32, (n, n), 1)
    return jnp.sum(jnp.where(here, row.astype(jnp.float32), 0.0), axis=1, keepdims=True)


def mirror_table(slot_row):
    n = slot_row.shape[1]
    slots = column(slot_row).astype(jnp.int32)
    return lax.broadcasted_iota(jnp.int32, (n, n), 1) == slots


class Rows:
    def __init__(self, rows, cols):
        self.rows = rows
        self.sorted = rows + IRREPS * CHUNK
        self.tiles = cols // TILE
        self.most = -(-rows // CHUNK)
        self.cap = self.tiles * self.most * 2 // 5
        self.energy = -(-rows // TILE)
        self.sent = (2 * self.cap + self.energy) * CHUNK


def list_chunks(shape, own, label_row, sizes, spots):
    firsts, first = [], jnp.int32(0)
    for g in range(IRREPS):
        count = jnp.sum(jnp.where(label_row == g, 1.0, 0.0)).astype(jnp.int32)
        chunks = (count + CHUNK - 1) // CHUNK
        sizes[g], sizes[IRREPS + g] = first, chunks
        firsts.append(first * CHUNK)
        first += chunks
    for n in range(shape.cap):
        spots[n] = 0
    total = jnp.int32(0)
    for j in range(shape.tiles):
        first, chunks = sizes[own[j]], sizes[IRREPS + own[j]]
        for c in range(shape.most):
            spots[total] = j * TILE + first + c
            total += (c < chunks).astype(jnp.int32)
    for n in range(shape.cap):
        spots[n] = jnp.where(n < total, spots[n], 0)
    return total, firsts


def first_of(labels, firsts):
    value = jnp.zeros(labels.shape, jnp.float32)
    for g, first in enumerate(firsts):
        value = jnp.where(labels == g, first.astype(jnp.float32), value)
    return value


def chunk_at(spot):
    return (
        pl.ds(pl.multiple_of(lax.rem(spot, TILE) * CHUNK, CHUNK), CHUNK),
        tile_at(spot // TILE),
    )


def rows_kernel(
    shape, own, amps_ref, driver_ref, label_row, energy_row, out_ref, full_ref, amps, drivers, sizes,
    spots,
):
    n = shape.rows
    total, firsts = list_chunks(shape, own, label_row[...], sizes, spots)
    full_ref[0] = (total > shape.cap).astype(jnp.int32)
    labels = column(label_row[...]).astype(jnp.int32)
    above = lax.broadcasted_iota(jnp.int32, (n, n), 0) < lax.broadcasted_iota(jnp.int32, (n, n), 1)
    rank = jnp.where((labels == label_row[...]) & above, 1.0, 0.0).sum(axis=0, keepdims=True)
    spot_row = (rank + first_of(label_row[...], firsts)).astype(jnp.int32)
    order = lax.broadcasted_iota(jnp.int32, (shape.sorted, n), 0) == spot_row
    order = order.astype(jnp.bfloat16)
    for to_ref, from_ref in ((amps, amps_ref), (drivers, driver_ref)):
        to_ref[...] = jnp.dot(order, from_ref[...], preferred_element_type=jnp.float32).astype(
            to_ref.dtype
        )
    for i in range(shape.cap):
        rows, cols = chunk_at(spots[i])
        out_ref[i * CHUNK : (i + 1) * CHUNK, :] = amps[rows, cols]
        out_ref[(shape.cap + i) * CHUNK : (shape.cap + i + 1) * CHUNK, :] = drivers[rows, cols]

    rest = jnp.broadcast_to(energy_row[...], (CHUNK, n))
    at = lax.broadcasted_iota(jnp.int32, (CHUNK, n), 0)
    terms = jnp.zeros((CHUNK, n), jnp.float32)
    for i in range(3):
        term = rest.astype(jnp.bfloat16).astype(jnp.float32)
        terms = jnp.where(at == i, term, terms)
        rest = rest - term
    for i in range(shape.energy):
        width = min(TILE, n - i * TILE)
        first = (2 * shape.cap + i) * CHUNK
        out_ref[first : first + CHUNK, :] = jnp.zeros((CHUNK, TILE), out_ref.dtype)
        out_ref[first : first + CHUNK, :width] = terms[:, i * TILE : i * TILE + width].astype(
            out_ref.dtype
        )


def mirror_kernel(shape, whole, own, amps_ref, bundle_ref, slot_row, label_row, energy_row, *refs):
    if whole:
        amps, drivers, after_ref, *cur_refs, mirror_driver_ref, columns_ref = refs
    else:
        after_ref, *cur_refs, mirror_driver_ref, columns_ref, amps, drivers, sizes, spots = refs
    rows = shape.rows
    table = mirror_table(slot_row[...])
    row_label = column(label_row[...])
    if whole:
        weights = table
    else:
        total, firsts = list_chunks(shape, own, label_row[...], sizes, spots)
        amps[...] = jnp.zeros_like(amps)
        drivers[...] = jnp.zeros_like(drivers)
        for i in range(shape.cap):
            at = chunk_at(spots[i])
            amps[at] = bundle_ref[i * CHUNK : (i + 1) * CHUNK, :]
            drivers[at] = bundle_ref[(shape.cap + i) * CHUNK : (shape.cap + i + 1) * CHUNK, :]
        slots = column(slot_row[...]).astype(jnp.int32)
        before = (row_label == label_row[...].astype(jnp.float32)) & (slot_row[...] < slots)
        rank = jnp.where(before, 1.0, 0.0).sum(axis=1, keepdims=True)
        spot = (rank + first_of(row_label, firsts)).astype(jnp.int32)
        weights = lax.broadcasted_iota(jnp.int32, (rows, shape.sorted), 1) == spot
    weights = weights.astype(jnp.bfloat16)
    mirrored = jnp.dot(weights, amps[...], preferred_element_type=jnp.float32)
    zero = jnp.zeros((), amps_ref.dtype)
    each = shape.tiles // PIECES
    for j in range(shape.tiles):
        cols = slice(j * TILE, (j + 1) * TILE)
        cur_ref, at = cur_refs[j // each], slice(j % each * TILE, (j % each + 1) * TILE)
        occupied = row_label == own[j].astype(jnp.float32)
        cur_ref[:rows, at] = jnp.where(occupied, amps_ref[:, cols], zero)
        cur_ref[rows:, at] = jnp.where(occupied, mirrored[:, cols], 0.0).astype(cur_ref.dtype)
    mirror_driver_ref[...] = jnp.dot(
        weights, drivers[...], preferred_element_type=jnp.float32
    ).astype(mirror_driver_ref.dtype)
    mirror_energy = jnp.zeros((rows, 1), jnp.float32)
    for i in range(shape.energy):
        width = min(TILE, rows - i * TILE)
        first = (2 * shape.cap + i) * CHUNK
        terms = bundle_ref[first : first + CHUNK, :width].astype(jnp.float32)
        other_energy = (terms[0:1] + terms[1:2]) + terms[2:3]
        here = table[:, i * TILE : i * TILE + width]
        mirror_energy += jnp.where(here, other_energy, 0.0).sum(axis=1, keepdims=True)
    for i, value in enumerate((row_label, column(energy_row[...]), mirror_energy)):
        columns_ref[i * rows : (i + 1) * rows, :] = jnp.broadcast_to(value, (rows, TILE))


def bounds(plan, place, core, first, count):
    del place
    return pl.ds(pl.multiple_of(core * plan.half * TILE + first, TILE), count)


def first_column(plan, place, i):
    here = lax.rem(place[0], plan.near)
    return lax.rem(here + 2 + i, plan.near) * plan.slab * TILE


def slot_of_near(plan, turn):
    return (-(turn // 2 + 1) - 2) % plan.near


def slot_of_far(plan, turn):
    return (-turn - 2) % plan.near


def turns_for(plan, slots):
    return (
        [t for t in range(2 * (plan.near - 1)) if slot_of_near(plan, t) in slots],
        [t for t in range(plan.near) if slot_of_far(plan, t) in slots],
    )


def fill(plan, slots, own, other, place, got, swapped, ints_ref, labels, spots):
    z, side, sub = place[0], place[1], place[2]
    here = lax.rem(z, plan.near)
    ints_ref[...] = jnp.zeros_like(ints_ref)
    all_labels(plan, own, other, sub, labels)
    near_turns, far_turns = turns_for(plan, slots)

    def put(slot, n, value):
        spot = spots[n]
        j, k = spot // plan.tiles, lax.rem(spot, plan.tiles)
        ints_ref[tile_at(k), tile_at((slot - slots[0]) * plan.slab + j)] = value

    def list_slot(slot):
        slab = sub * plan.near + lax.rem(here + 2 + slot, plan.near)
        list_tiles(plan, labels, slab, spots)

    @pl.when(z // plan.near == sub)
    def _():
        for turn in near_turns:
            slot = slot_of_near(plan, turn)
            if turn % 2 == 0:
                list_slot(slot)
            for n in range(plan.part):
                put(slot, turn % 2 * plan.part + n, got[turn][n * TILE : (n + 1) * TILE, :])

    @pl.when(z // plan.near != sub)
    def _():
        for turn in far_turns:
            slot = slot_of_far(plan, turn)
            list_slot(slot)
            for n in range(plan.part):
                rows = slice(n * TILE, (n + 1) * TILE)
                put(slot, side * plan.part + n, got[turn][rows, :])
                put(slot, (1 - side) * plan.part + n, swapped[turn][rows, :])


def new_current(plan, slots, own, place, pieces, ints_ref, driver, mirror_driver, columns, col_energy,
                cur_ref):
    rows = driver.shape[0]
    width = plan.slab * TILE
    wide = min(width, 2 * TILE)
    terms = []
    for i, piece in enumerate(pieces):
        core = place[2] if i < PIECES else 1 - place[2]
        count = plan.half * TILE // PIECES
        terms.append((piece, bounds(plan, place, core, i % PIECES * count, count)))
    for slot in slots:
        first = first_column(plan, place, slot)
        for c in range(0, width, wide):
            cols = slice((slot - slots[0]) * width + c, (slot - slots[0]) * width + c + wide)
            total = None
            for piece, at in terms:
                term = jnp.dot(piece[...], ints_ref[at, cols], preferred_element_type=jnp.float32)
                total = term if total is None else total + term
            sym = total[:rows] + total[rows:]
            for t in range(0, wide, TILE):
                at = pl.ds(pl.multiple_of(first + c + t, TILE), TILE)
                label = own[(first + c + t) // TILE].astype(jnp.float32)
                occupied = columns[:rows] == label
                for i, source in enumerate((driver, mirror_driver)):
                    gap = col_energy[:, at] - columns[(i + 1) * rows : (i + 2) * rows]
                    new = (source[:, at].astype(jnp.float32) + sym[:, t : t + TILE]) / gap
                    new = jnp.where(occupied, new, 0.0)
                    cur_ref[i * rows : (i + 1) * rows, cols.start + t : cols.start + t + TILE] = (
                        new.astype(cur_ref.dtype)
                    )


def early_kernel(plan, turns, *refs):
    own, other, place, mine_ref, their_ref = refs[:5]
    pieces, refs = refs[5 : 5 + 2 * PIECES], refs[5 + 2 * PIECES :]
    driver, mirror_driver, columns, col_energy = refs[:4]
    got = dict(zip(turns[0], refs[4:]))
    swapped = dict(zip(turns[1], refs[4 + len(turns[0]) :]))
    ints_ref, cur_ref, labels, spots = refs[-4:]
    slots = range(plan.near - 1)
    width = plan.slab * TILE
    fill(plan, slots, own, other, place, got, swapped, ints_ref, labels, spots)

    @pl.when(place[0] // plan.near == place[2])
    def _():
        cols = slice((plan.near - 2) * width, (plan.near - 1) * width)
        ints_ref[bounds(plan, place, place[2], 0, plan.half * TILE), cols] = mine_ref[...]
        ints_ref[bounds(plan, place, 1 - place[2], 0, plan.half * TILE), cols] = their_ref[...]

    new_current(plan, slots, own, place, pieces, ints_ref, driver, mirror_driver, columns, col_energy,
                cur_ref)


def late_kernel(plan, turns, *refs):
    own, other, place = refs[:3]
    pieces, refs = refs[3 : 3 + 2 * PIECES], refs[3 + 2 * PIECES :]
    driver, mirror_driver, columns, col_energy = refs[:4]
    got = dict(zip(turns[0], refs[4:]))
    swapped = dict(zip(turns[1], refs[4 + len(turns[0]) :]))
    ints_ref, cur_ref, labels, spots = refs[-4:]
    slots = range(plan.near - 1, plan.near)
    fill(plan, slots, own, other, place, got, swapped, ints_ref, labels, spots)
    new_current(plan, slots, own, place, pieces, ints_ref, driver, mirror_driver, columns, col_energy,
                cur_ref)


def product(plan, place, terms, ints_ref, cols):
    width = plan.slab * TILE
    total = None
    for cur_ref, core, slots in terms:
        for slot in slots:
            at = slice((slot - slots[0]) * width, (slot - slots[0] + 1) * width)
            rows = bounds(plan, place, core, first_column(plan, place, slot), width)
            term = jnp.dot(
                cur_ref[:, at], ints_ref[rows, cols], preferred_element_type=jnp.float32
            )
            total = term if total is None else total + term
    half = total.shape[0] // 2
    return total[:half] + total[half:]


def blocks(plan, count):
    width = plan.slab * TILE
    wide = min(width, 2 * TILE)
    return [slice(c, c + wide) for c in range(0, count * width, wide)]


def early_part_kernel(plan, place, a_mine, a_their, ints_a, sym_ref):
    a = range(plan.near - 1)
    terms = [(a_mine, place[2], a), (a_their, 1 - place[2], a)]
    for cols in blocks(plan, plan.near - 1):
        sym_ref[:, cols] = product(plan, place, terms, ints_a, cols)


def part_kernel(plan, place, a_mine, a_their, b_mine, ints_a, ints_b, early_ref, sym_ref):
    a, b = range(plan.near - 1), range(plan.near - 1, plan.near)
    terms = [(b_mine, place[2], b)]
    for cols in blocks(plan, plan.near - 1):
        sym_ref[:, cols] = early_ref[:, cols] + product(plan, place, terms, ints_a, cols)
    terms = [(a_mine, place[2], a), (a_their, 1 - place[2], a), (b_mine, place[2], b)]
    width = (plan.near - 1) * plan.slab * TILE
    for cols in blocks(plan, 1):
        sym_ref[:, width + cols.start : width + cols.stop] = product(plan, place, terms, ints_b, cols)


def last_kernel(plan, own, place, b_their, ints_a, ints_b, sym_ref, driver, columns, col_energy, out_ref,
                new_ref, sems):
    rows = driver.shape[0]
    terms = [(b_their, 1 - place[2], range(plan.near - 1, plan.near))]
    width = plan.slab * TILE
    copies = []
    for c, cols in enumerate(blocks(plan, plan.near)):
        slot = cols.start // width
        ints_ref, start = (ints_b, cols.start - slot * width) if slot == plan.near - 1 else (ints_a, cols.start)
        wide = cols.stop - cols.start
        sym = sym_ref[:, cols] + product(plan, place, terms, ints_ref, slice(start, start + wide))
        first = first_column(plan, place, slot) + cols.start - slot * width
        for t in range(0, wide, TILE):
            at = pl.ds(pl.multiple_of(first + t, TILE), TILE)
            occupied = columns[:rows] == own[(first + t) // TILE].astype(jnp.float32)
            gap = col_energy[:, at] - columns[rows : 2 * rows]
            new = (driver[:, at].astype(jnp.float32) + sym[:, t : t + TILE]) / gap
            new_ref[:, cols.start + t : cols.start + t + TILE] = jnp.where(occupied, new, 0.0)
        copy = pltpu.make_async_copy(
            new_ref.at[:, cols],
            out_ref.at[:, pl.ds(pl.multiple_of(first, TILE), wide)],
            sems.at[c],
        )
        copy.start()
        copies.append(copy)
    for copy in copies:
        copy.wait()


def call(kernel, smem, vmem, outs, scratch=(), anywhere=(), flag=False, flops=0, to_hbm=False):
    moved = sum(v.size * v.dtype.itemsize for v in vmem)
    in_smem, in_vmem = pl.BlockSpec(memory_space=pltpu.SMEM), pl.BlockSpec(memory_space=pltpu.VMEM)
    in_any = pl.BlockSpec(memory_space=pl.ANY)
    return pl.pallas_call(
        kernel,
        out_shape=list(outs) + [jax.ShapeDtypeStruct((1,), jnp.int32)] * flag,
        in_specs=[in_smem] * len(smem) + [in_vmem] * len(vmem) + [in_any] * len(anywhere),
        out_specs=[pl.BlockSpec(memory_space=pltpu.HBM) if to_hbm else in_vmem] * len(outs) + [in_smem] * flag,
        scratch_shapes=scratch,
        compiler_params=pltpu.CompilerParams(vmem_limit_bytes=VMEM_BYTES),
        cost_estimate=pl.CostEstimate(flops=0, bytes_accessed=0, transcendentals=0),
    )(*smem, *vmem, *anywhere)


def body(
    amplitudes, driver, integrals, pair_energy, col_energy, tile_irrep, pair_irrep, mirror_slot
):
    places, sides = lax.axis_size("virt"), lax.axis_size("pair")
    partner_bit = sides.bit_length() - 2
    rows, half_cols = amplitudes.shape
    slab_tiles = integrals.shape[1] // TILE
    plans = [
        Plan(2 * half_cols // TILE, slab_tiles, places, per_tile * slab_tiles)
        for per_tile in CAPS
    ]
    plan = plans[-1]
    z, sub = lax.axis_index("virt"), lax.axis_index("sub")
    side = (lax.axis_index("pair") >> partner_bit) & 1
    place = jnp.stack([z, side, sub]).astype(jnp.int32)

    def like(shape, dtype=integrals.dtype):
        return jax.ShapeDtypeStruct(shape, dtype)

    other_irrep = from_partner(tile_irrep, "sub", 0)
    their_ints = from_partner(integrals, "sub", 0)

    label_row, slot_row, energy_row = pair_irrep[None, :], mirror_slot[None, :], pair_energy[None, :]
    shape = Rows(rows, half_cols)
    sort_scratch = [pltpu.VMEM((shape.sorted, half_cols), amplitudes.dtype)] * 2 + [
        pltpu.SMEM((2 * IRREPS,), jnp.int32),
        pltpu.SMEM((shape.tiles * shape.most + 1,), jnp.int32),
    ]
    bundle, rows_full = call(
        functools.partial(rows_kernel, shape),
        (tile_irrep,),
        (amplitudes, driver, label_row, energy_row),
        [like((shape.sent, TILE))],
        sort_scratch,
        flag=True,
    )

    lists = [pltpu.SMEM((plan.tiles,), jnp.int32), pltpu.SMEM((plan.slab * plan.tiles + 1,), jnp.int32)]
    *sends, level = call(
        functools.partial(pack_kernel, plans),
        (tile_irrep, other_irrep, place),
        (integrals, their_ints),
        [like((each.part * TILE, TILE)) for each in plans for _ in range(2)],
        lists + [pltpu.SMEM((plan.tiles,), jnp.int32)],
        anywhere=(bundle,),
        flag=True,
    )

    def sparse(index):
        return sparse_plan(
            plans[index], sends[2 * index : 2 * index + 2], place, lists, shape, sort_scratch,
            other_irrep, their_ints, bundle, rows_full, amplitudes, driver, integrals, label_row,
            slot_row, energy_row, col_energy, tile_irrep,
        )

    def dense():
        return dense_plan(
            amplitudes, driver, integrals, pair_energy, col_energy, tile_irrep, pair_irrep,
            mirror_slot,
        )

    branches = [functools.partial(sparse, index) for index in range(len(plans))] + [dense]
    return lax.switch(level[0], branches)


def sparse_plan(
    plan, sends, place, lists, shape, sort_scratch, other_irrep, their_ints, bundle, rows_full,
    amplitudes, driver, integrals, label_row, slot_row, energy_row, col_energy, tile_irrep,
):
    places, sides = lax.axis_size("virt"), lax.axis_size("pair")
    partner_bit = sides.bit_length() - 2
    rows, half_cols = amplitudes.shape

    def like(shape, dtype=integrals.dtype):
        return jax.ShapeDtypeStruct(shape, dtype)

    def over_pair(value):
        return from_partner(value, "pair", partner_bit)

    near = plan.near
    got = []
    for turn in range(max(2 * (near - 1), near)):
        pairs = []
        for i in range(places):
            half, at = i // near, i % near
            if turn < 2 * (near - 1):
                to = half * near + (at + turn // 2 + 1) % near
                pairs.append((2 * i + half, 2 * to + half))
            if turn < near:
                to = (1 - half) * near + (at + turn) % near
                pairs.append((2 * i + 1 - half, 2 * to + half))
        got.append(lax.ppermute(sends[turn % 2], ("virt", "sub"), pairs))
    pairs = []
    for i in range(places):
        for j in range(sides):
            far = 1 - i // near
            pairs.append(((i * sides + j) * 2 + far, (i * sides + (j ^ 1 << partner_bit)) * 2 + far))
    swapped = [lax.ppermute(value, ("virt", "pair", "sub"), pairs) for value in got[:near]]

    other_bundle = over_pair(bundle)
    def mirror(whole, more=()):
        return tuple(call(
            functools.partial(mirror_kernel, shape, whole),
            (tile_irrep,),
            (amplitudes, other_bundle, slot_row, label_row, energy_row, *more),
            [like((2 * rows, half_cols // PIECES))] * PIECES
            + [like((rows, half_cols)), like((3 * rows, TILE), jnp.float32)],
            () if whole else sort_scratch,
            anywhere=(bundle,),
        ))

    *cur_mine, mirror_driver, columns = lax.cond(
        rows_full[0] > 0,
        lambda: mirror(True, (over_pair(amplitudes), over_pair(driver))),
        lambda: mirror(False),
    )
    cur_their = [from_partner(piece, "sub", 0) for piece in cur_mine]

    energy = col_energy[None, :]
    width = plan.slab * TILE
    near_cols, flops = (near - 1) * width, 2 * 2 * rows * plan.tiles * TILE * width
    common = (*cur_mine, *cur_their, driver, mirror_driver, columns, energy)

    turns = turns_for(plan, range(near - 1))
    turns = (sorted({*turns[0], *turns[1]}), turns[1])
    ints_a, a_mine = call(
        functools.partial(early_kernel, plan, turns),
        (tile_irrep, other_irrep, place),
        (integrals, their_ints, *common, *[got[t] for t in turns[0]], *[swapped[t] for t in turns[1]]),
        [like((plan.tiles * TILE, near_cols)), like((2 * rows, near_cols))],
        lists,
        flops=flops * (near - 1),
    )
    a_their = from_partner(a_mine, "sub", 0)
    (early,) = call(
        functools.partial(early_part_kernel, plan),
        (place,),
        (a_mine, a_their, ints_a),
        [like((rows, near_cols), jnp.float32)],
        flops=flops // 2,
    )
    turns = turns_for(plan, range(near - 1, near))
    turns = (sorted({*turns[0], *turns[1]}), turns[1])
    ints_b, b_mine = call(
        functools.partial(late_kernel, plan, turns),
        (tile_irrep, other_irrep, place),
        (*common, *[got[t] for t in turns[0]], *[swapped[t] for t in turns[1]]),
        [like((plan.tiles * TILE, width)), like((2 * rows, width))],
        lists,
        flops=flops,
    )
    b_their = from_partner(b_mine, "sub", 0)
    (sym,) = call(
        functools.partial(part_kernel, plan),
        (place,),
        (a_mine, a_their, b_mine, ints_a, ints_b, early),
        [like((rows, half_cols), jnp.float32)],
        flops=flops,
    )
    return call(
        functools.partial(last_kernel, plan),
        (tile_irrep, place),
        (b_their, ints_a, ints_b, sym, driver, columns, energy),
        [like((rows, half_cols), jnp.float32)],
        [pltpu.VMEM((rows, half_cols), jnp.float32),
         pltpu.SemaphoreType.DMA((len(blocks(plan, near)),))],
        flops=flops // 2,
        to_hbm=True,
    )[0]


def solution(mesh):
    return jax.shard_map(
        body,
        mesh=mesh,
        in_specs=(
            P(("groups", "pair", "virt"), "sub"),
            P(("groups", "pair", "virt"), "sub"),
            P(("groups", "sub"), "virt"),
            P(("groups", "pair", "virt")),
            P(("groups", "sub")),
            P(("groups", "sub")),
            P(("groups", "pair", "virt")),
            P(("groups", "pair", "virt")),
        ),
        out_specs=P(("groups", "pair", "virt"), "sub"),
        check_vma=False,
    )
```

```python
import functools

import jax
import jax.numpy as jnp
from jax import lax
from jax.experimental import pallas as pl
from jax.experimental.pallas import tpu as pltpu
from jax.sharding import PartitionSpec as P

ITERS = 2
TILE = 128
IRREPS = 4
PIECES = 2
CHUNK = 16
CAPS = (6, 7, 8)
VMEM_BYTES = 20 * 1024 * 1024


def from_partner(value, axis, apart):
    return lax.ppermute(value, axis, [(i, i ^ 1 << apart) for i in range(lax.axis_size(axis))])


def contract(blocks, integrals):
    places, z, sub = lax.axis_size("virt"), lax.axis_index("virt"), lax.axis_index("sub")
    width = integrals.shape[1]
    whole = jnp.zeros((integrals.shape[0], places * width), integrals.dtype)
    for apart in range(places):
        slab = integrals
        if apart:
            slab = lax.ppermute(
                integrals, "virt", [(i, (i + apart) % places) for i in range(places)]
            )
        at = lax.rem(z - apart + places, places) * width
        whole = lax.dynamic_update_slice(whole, slab, (0, at))
    total = jnp.dot(blocks[0], whole, preferred_element_type=jnp.float32)
    half = total.shape[1] // 2
    mine = lax.dynamic_slice_in_dim(total, sub * half, half, 1)
    theirs = lax.dynamic_slice_in_dim(total, (1 - sub) * half, half, 1)
    return mine + from_partner(theirs, "sub", 0)


def dense_plan(
    amplitudes, driver, integrals, pair_energy, col_energy, tile_irrep, pair_irrep, mirror_slot
):
    col_irrep = jnp.repeat(tile_irrep, TILE)
    occupied = pair_irrep[:, None] == col_irrep[None, :]
    energy_gap = col_energy[None, :] - pair_energy[:, None]
    driver_wide = driver.astype(jnp.float32)
    partner_bit = lax.axis_size("pair").bit_length() - 2
    current = jnp.where(occupied, amplitudes, jnp.zeros((), amplitudes.dtype))
    updated = driver_wide
    for iteration in range(ITERS):
        ladder = contract((current,), integrals)
        mirror_block = from_partner(ladder, "pair", partner_bit)
        symmetric = ladder + jnp.take(mirror_block, mirror_slot, axis=0)
        updated = jnp.where(
            occupied, (driver_wide + symmetric) / energy_gap, jnp.zeros((), jnp.float32)
        )
        current = updated.astype(jnp.bfloat16)
    return updated


class Plan:
    def __init__(self, tiles, slab_tiles, places, cap):
        self.tiles = tiles
        self.half = tiles // 2
        self.slab = slab_tiles
        self.places = places
        self.near = places // 2
        self.part = -(-cap // 2)
        self.cap = 2 * self.part

    def pieces(self, rows):
        first = max(self.half // 2, self.part * TILE // rows + 1)
        return (first, self.half - first)


def split(value, size):
    assert size & (size - 1) == 0
    return value >> (size.bit_length() - 1), value & (size - 1)


def tile_at(index):
    return pl.ds(pl.multiple_of(index * TILE, TILE), TILE)


def all_labels(plan, own, other, sub, labels):
    for i in range(plan.half):
        labels[sub * plan.half + i] = own[i]
        labels[(1 - sub) * plan.half + i] = other[i]


def list_tiles(plan, labels, slab, spots):
    for n in range(plan.cap):
        spots[n] = 0
    count = jnp.int32(0)
    for j in range(plan.slab):
        here = labels[slab * plan.slab + j]
        for k in range(plan.tiles):
            spots[count] = j * plan.tiles + k
            count += (labels[k] == here).astype(jnp.int32)
    spots[count] = 0


def list_kernel(plans, own, other, place, level_ref, spots_ref, labels, spots, sizes):
    plan = plans[-1]
    all_labels(plan, own, other, place[2], labels)
    for k in range(plan.tiles):
        sizes[k] = 0
    for k in range(plan.tiles):
        sizes[labels[k]] += 1
    most = jnp.int32(0)
    for i in range(plan.places):
        needed = jnp.int32(0)
        for j in range(plan.slab):
            needed += sizes[labels[i * plan.slab + j]]
        most = jnp.maximum(most, needed)
    level = jnp.int32(0)
    for each in plans:
        level += (most > each.cap).astype(jnp.int32)
    level_ref[0] = level
    list_tiles(plan, labels, place[0], spots)
    for n in range(plan.cap):
        spots_ref[n] = spots[n]


def pack_kernel(plan, spots, place, mine_ref, their_ref, *send_refs):
    slab, side, sub = place[0], place[1], place[2]
    is_near = slab // plan.near == sub
    for i, to_ref in enumerate(send_refs):
        first = jnp.where(is_near, i, side) * plan.part
        for n in range(plan.part):
            spot = spots[first + n]
            j, k = split(spot, plan.tiles)
            core, row = split(k, plan.half)
            rows, cols = tile_at(row), tile_at(j)
            to_ref[n * TILE : (n + 1) * TILE, :] = jnp.where(
                core == sub, mine_ref[rows, cols], their_ref[rows, cols]
            )


def column(row):
    n = row.shape[1]
    here = lax.broadcasted_iota(jnp.int32, (n, n), 0) == lax.broadcasted_iota(jnp.int32, (n, n), 1)
    return jnp.sum(jnp.where(here, row.astype(jnp.float32), 0.0), axis=1, keepdims=True)


def mirror_table(slot_row):
    n = slot_row.shape[1]
    slots = column(slot_row).astype(jnp.int32)
    return lax.broadcasted_iota(jnp.int32, (n, n), 1) == slots


class Rows:
    def __init__(self, rows, cols):
        self.rows = rows
        self.sorted = rows + IRREPS * CHUNK
        self.tiles = cols // TILE
        self.most = -(-rows // CHUNK)
        self.cap = self.tiles * self.most * 2 // 5
        self.energy = -(-rows // TILE)
        self.sent = (2 * self.cap + self.energy) * CHUNK


def list_chunks(shape, own, label_row, sizes, spots):
    firsts, first = [], jnp.int32(0)
    for g in range(IRREPS):
        count = jnp.sum(jnp.where(label_row == g, 1.0, 0.0)).astype(jnp.int32)
        chunks = (count + CHUNK - 1) // CHUNK
        sizes[g], sizes[IRREPS + g] = first, chunks
        firsts.append(first * CHUNK)
        first += chunks
    for n in range(shape.cap):
        spots[n] = 0
    total = jnp.int32(0)
    for j in range(shape.tiles):
        first, chunks = sizes[own[j]], sizes[IRREPS + own[j]]
        for c in range(shape.most):
            spots[total] = j * TILE + first + c
            total += (c < chunks).astype(jnp.int32)
    spots[total] = 0
    return total, firsts


def first_of(labels, firsts):
    value = jnp.zeros(labels.shape, jnp.float32)
    for g, first in enumerate(firsts):
        value = jnp.where(labels == g, first.astype(jnp.float32), value)
    return value


def chunk_at(spot):
    j, chunk = split(spot, TILE)
    return pl.ds(pl.multiple_of(chunk * CHUNK, CHUNK), CHUNK), tile_at(j)


def rows_kernel(
    shape, own, amps_ref, driver_ref, label_row, energy_row, out_ref, full_ref, amps, drivers, sizes,
    spots,
):
    n = shape.rows
    total, firsts = list_chunks(shape, own, label_row[...], sizes, spots)
    full_ref[0] = (total > shape.cap).astype(jnp.int32)
    labels = column(label_row[...]).astype(jnp.int32)
    above = lax.broadcasted_iota(jnp.int32, (n, n), 0) < lax.broadcasted_iota(jnp.int32, (n, n), 1)
    rank = jnp.where((labels == label_row[...]) & above, 1.0, 0.0).sum(axis=0, keepdims=True)
    spot_row = (rank + first_of(label_row[...], firsts)).astype(jnp.int32)
    order = lax.broadcasted_iota(jnp.int32, (shape.sorted, n), 0) == spot_row
    order = order.astype(jnp.bfloat16)
    for to_ref, from_ref in ((amps, amps_ref), (drivers, driver_ref)):
        to_ref[...] = jnp.dot(order, from_ref[...], preferred_element_type=jnp.float32).astype(
            to_ref.dtype
        )
    for i in range(shape.cap):
        rows, cols = chunk_at(spots[i])
        out_ref[i * CHUNK : (i + 1) * CHUNK, :] = amps[rows, cols]
        out_ref[(shape.cap + i) * CHUNK : (shape.cap + i + 1) * CHUNK, :] = drivers[rows, cols]

    rest = jnp.broadcast_to(energy_row[...], (CHUNK, n))
    at = lax.broadcasted_iota(jnp.int32, (CHUNK, n), 0)
    terms = jnp.zeros((CHUNK, n), jnp.float32)
    for i in range(3):
        term = rest.astype(jnp.bfloat16).astype(jnp.float32)
        terms = jnp.where(at == i, term, terms)
        rest = rest - term
    for i in range(shape.energy):
        width = min(TILE, n - i * TILE)
        first = (2 * shape.cap + i) * CHUNK
        out_ref[first : first + CHUNK, :] = jnp.zeros((CHUNK, TILE), out_ref.dtype)
        out_ref[first : first + CHUNK, :width] = terms[:, i * TILE : i * TILE + width].astype(
            out_ref.dtype
        )


def mirror_kernel(shape, pieces, whole, own, amps_ref, bundle_ref, slot_row, label_row, energy_row, *refs):
    if whole:
        amps, drivers, *cur_refs, mirror_driver_ref, columns_ref = refs
    else:
        *cur_refs, mirror_driver_ref, columns_ref, amps, drivers, sizes, spots = refs
    rows = shape.rows
    table = mirror_table(slot_row[...])
    row_label = column(label_row[...])
    if whole:
        weights = table
    else:
        total, firsts = list_chunks(shape, own, label_row[...], sizes, spots)
        amps[...] = jnp.zeros_like(amps)
        drivers[...] = jnp.zeros_like(drivers)
        for i in range(shape.cap):
            at = chunk_at(spots[i])
            amps[at] = bundle_ref[i * CHUNK : (i + 1) * CHUNK, :]
            drivers[at] = bundle_ref[(shape.cap + i) * CHUNK : (shape.cap + i + 1) * CHUNK, :]
        slots = column(slot_row[...]).astype(jnp.int32)
        before = (row_label == label_row[...].astype(jnp.float32)) & (slot_row[...] < slots)
        rank = jnp.where(before, 1.0, 0.0).sum(axis=1, keepdims=True)
        spot = (rank + first_of(row_label, firsts)).astype(jnp.int32)
        weights = lax.broadcasted_iota(jnp.int32, (rows, shape.sorted), 1) == spot
    weights = weights.astype(jnp.bfloat16)
    mirrored = jnp.dot(weights, amps[...], preferred_element_type=jnp.float32)
    zero = jnp.zeros((), amps_ref.dtype)
    for j in range(shape.tiles):
        cols = slice(j * TILE, (j + 1) * TILE)
        cur_ref, first = (cur_refs[0], 0) if j < pieces[0] else (cur_refs[1], pieces[0])
        at = slice((j - first) * TILE, (j - first + 1) * TILE)
        occupied = row_label == own[j].astype(jnp.float32)
        cur_ref[:rows, at] = jnp.where(occupied, amps_ref[:, cols], zero)
        cur_ref[rows:, at] = jnp.where(occupied, mirrored[:, cols], 0.0).astype(cur_ref.dtype)
    mirror_driver_ref[...] = jnp.dot(
        weights, drivers[...], preferred_element_type=jnp.float32
    ).astype(mirror_driver_ref.dtype)
    mirror_energy = jnp.zeros((rows, 1), jnp.float32)
    for i in range(shape.energy):
        width = min(TILE, rows - i * TILE)
        first = (2 * shape.cap + i) * CHUNK
        terms = bundle_ref[first : first + CHUNK, :width].astype(jnp.float32)
        other_energy = (terms[0:1] + terms[1:2]) + terms[2:3]
        here = table[:, i * TILE : i * TILE + width]
        mirror_energy += jnp.where(here, other_energy, 0.0).sum(axis=1, keepdims=True)
    for i, value in enumerate((row_label, column(energy_row[...]), mirror_energy)):
        columns_ref[i * rows : (i + 1) * rows, :] = jnp.broadcast_to(value, (rows, TILE))


def bounds(plan, core, first, count):
    return pl.ds(pl.multiple_of(core * plan.half * TILE + first, TILE), count)


def first_column(plan, place, i):
    here = lax.rem(place[0], plan.near)
    return lax.rem(here + 2 + i, plan.near) * plan.slab * TILE


def slot_of_near(plan, turn):
    return (-(turn // 2 + 1) - 2) % plan.near


def slot_of_far(plan, turn):
    return (-turn - 2) % plan.near


def turns_for(plan, slots):
    return (
        [t for t in range(2 * (plan.near - 1)) if slot_of_near(plan, t) in slots],
        [t for t in range(plan.near) if slot_of_far(plan, t) in slots],
    )


def fill(plan, slots, own, other, place, near_got, far_got, swapped, ints_ref, labels, spots):
    z, side, sub = place[0], place[1], place[2]
    here = lax.rem(z, plan.near)
    ints_ref[...] = jnp.zeros_like(ints_ref)
    all_labels(plan, own, other, sub, labels)
    near_turns, far_turns = turns_for(plan, slots)

    def put(slot, n, value):
        spot = spots[n]
        j, k = split(spot, plan.tiles)
        ints_ref[tile_at(k), tile_at((slot - slots[0]) * plan.slab + j)] = value

    def list_slot(slot):
        slab = sub * plan.near + lax.rem(here + 2 + slot, plan.near)
        list_tiles(plan, labels, slab, spots)

    @pl.when(z // plan.near == sub)
    def _():
        for turn in near_turns:
            slot = slot_of_near(plan, turn)
            if turn % 2 == 0:
                list_slot(slot)
            for n in range(plan.part):
                tile = near_got[turn][n * TILE : (n + 1) * TILE, :]
                put(slot, turn % 2 * plan.part + n, tile)

    @pl.when(z // plan.near != sub)
    def _():
        for turn in far_turns:
            slot = slot_of_far(plan, turn)
            list_slot(slot)
            for n in range(plan.part):
                rows = slice(n * TILE, (n + 1) * TILE)
                put(slot, side * plan.part + n, far_got[turn][rows, :])
                put(slot, (1 - side) * plan.part + n, swapped[turn][rows, :])


def new_current(plan, slots, own, place, pieces, ints_ref, driver, mirror_driver, columns, col_energy,
                cur_ref):
    rows = driver.shape[0]
    width = plan.slab * TILE
    wide = min(width, 2 * TILE)
    terms = []
    for i, piece in enumerate(pieces):
        core = place[2] if i < PIECES else 1 - place[2]
        sizes = [tiles * TILE for tiles in plan.pieces(2 * rows)]
        terms.append((piece, bounds(plan, core, i % PIECES * sizes[0], sizes[i % PIECES])))
    for slot in slots:
        first = first_column(plan, place, slot)
        for c in range(0, width, wide):
            cols = slice((slot - slots[0]) * width + c, (slot - slots[0]) * width + c + wide)
            total = None
            for piece, at in terms:
                term = jnp.dot(piece[...], ints_ref[at, cols], preferred_element_type=jnp.float32)
                total = term if total is None else total + term
            sym = total[:rows] + total[rows:]
            for t in range(0, wide, TILE):
                at = pl.ds(pl.multiple_of(first + c + t, TILE), TILE)
                occupied = columns[:rows] == own[(first + c + t) // TILE].astype(jnp.float32)
                for i, source in enumerate((driver, mirror_driver)):
                    gap = col_energy[:, at] - columns[(i + 1) * rows : (i + 2) * rows]
                    new = (source[:, at].astype(jnp.float32) + sym[:, t : t + TILE]) / gap
                    new = jnp.where(occupied, new, 0.0)
                    cur_ref[i * rows : (i + 1) * rows, cols.start + t : cols.start + t + TILE] = (
                        new.astype(cur_ref.dtype)
                    )


def take_turns(turns, refs):
    refs = list(refs)
    return [{t: refs.pop(0) for t in each} for each in (turns[0], turns[1], turns[1])]


def early_kernel(plan, turns, *refs):
    own, other, place, mine_ref, their_ref = refs[:5]
    pieces, refs = refs[5 : 5 + 2 * PIECES], refs[5 + 2 * PIECES :]
    came = take_turns(turns, refs[4:-4])
    ints_ref, cur_ref, labels, spots = refs[-4:]
    slots = range(plan.near - 1)
    width = plan.slab * TILE
    fill(plan, slots, own, other, place, *came, ints_ref, labels, spots)

    @pl.when(place[0] // plan.near == place[2])
    def _():
        cols = slice((plan.near - 2) * width, (plan.near - 1) * width)
        ints_ref[bounds(plan, place[2], 0, plan.half * TILE), cols] = mine_ref[...]
        ints_ref[bounds(plan, 1 - place[2], 0, plan.half * TILE), cols] = their_ref[...]

    new_current(plan, slots, own, place, pieces, ints_ref, *refs[:4], cur_ref)


def late_kernel(plan, turns, *refs):
    own, other, place = refs[:3]
    pieces, refs = refs[3 : 3 + 2 * PIECES], refs[3 + 2 * PIECES :]
    came = take_turns(turns, refs[4:-4])
    ints_ref, cur_ref, labels, spots = refs[-4:]
    slots = range(plan.near - 1, plan.near)
    fill(plan, slots, own, other, place, *came, ints_ref, labels, spots)
    new_current(plan, slots, own, place, pieces, ints_ref, *refs[:4], cur_ref)


def product(plan, place, terms, ints_ref, cols):
    width = plan.slab * TILE
    total = None
    for cur_ref, core, slots in terms:
        for slot in slots:
            at = slice((slot - slots[0]) * width, (slot - slots[0] + 1) * width)
            rows = bounds(plan, core, first_column(plan, place, slot), width)
            term = jnp.dot(
                cur_ref[:, at], ints_ref[rows, cols], preferred_element_type=jnp.float32
            )
            total = term if total is None else total + term
    half = total.shape[0] // 2
    return total[:half] + total[half:]


def blocks(plan, count):
    width = plan.slab * TILE
    wide = min(width, 2 * TILE)
    return [slice(c, c + wide) for c in range(0, count * width, wide)]


def early_part_kernel(plan, place, a_mine, a_their, ints_a, sym_ref):
    a = range(plan.near - 1)
    terms = [(a_mine, place[2], a), (a_their, 1 - place[2], a)]
    for cols in blocks(plan, plan.near - 1):
        sym_ref[:, cols] = product(plan, place, terms, ints_a, cols)


def part_kernel(plan, place, a_mine, a_their, b_mine, ints_a, ints_b, early_ref, sym_ref):
    a, b = range(plan.near - 1), range(plan.near - 1, plan.near)
    terms = [(b_mine, place[2], b)]
    for cols in blocks(plan, plan.near - 1):
        sym_ref[:, cols] = early_ref[:, cols] + product(plan, place, terms, ints_a, cols)
    terms = [(a_mine, place[2], a), (a_their, 1 - place[2], a), (b_mine, place[2], b)]
    width = (plan.near - 1) * plan.slab * TILE
    for cols in blocks(plan, 1):
        sym_ref[:, width + cols.start : width + cols.stop] = product(plan, place, terms, ints_b, cols)


def last_kernel(plan, own, place, b_their, ints_a, ints_b, sym_ref, driver, columns, col_energy, out_ref,
                new_ref, sems):
    rows = driver.shape[0]
    terms = [(b_their, 1 - place[2], range(plan.near - 1, plan.near))]
    width = plan.slab * TILE
    copies = []
    for c, cols in enumerate(blocks(plan, plan.near)):
        slot = cols.start // width
        ints_ref, start = (ints_b, cols.start - slot * width) if slot == plan.near - 1 else (ints_a, cols.start)
        wide = cols.stop - cols.start
        sym = sym_ref[:, cols] + product(plan, place, terms, ints_ref, slice(start, start + wide))
        first = first_column(plan, place, slot) + cols.start - slot * width
        for t in range(0, wide, TILE):
            at = pl.ds(pl.multiple_of(first + t, TILE), TILE)
            occupied = columns[:rows] == own[(first + t) // TILE].astype(jnp.float32)
            gap = col_energy[:, at] - columns[rows : 2 * rows]
            new = (driver[:, at].astype(jnp.float32) + sym[:, t : t + TILE]) / gap
            new_ref[:, cols.start + t : cols.start + t + TILE] = jnp.where(occupied, new, 0.0)
        at = pl.ds(pl.multiple_of(first, TILE), wide)
        copy = pltpu.make_async_copy(new_ref.at[:, cols], out_ref.at[:, at], sems.at[c])
        copy.start()
        copies.append(copy)
    for copy in copies:
        copy.wait()


def call(kernel, smem, vmem, outs, scratch=(), anywhere=(), flag=False, flops=0, to_hbm=False):
    moved = sum(v.size * v.dtype.itemsize for v in vmem)
    in_smem, in_vmem = pl.BlockSpec(memory_space=pltpu.SMEM), pl.BlockSpec(memory_space=pltpu.VMEM)
    in_any = pl.BlockSpec(memory_space=pl.ANY)
    return pl.pallas_call(
        kernel,
        out_shape=list(outs) + [jax.ShapeDtypeStruct((1,), jnp.int32)] * flag,
        in_specs=[in_smem] * len(smem) + [in_vmem] * len(vmem) + [in_any] * len(anywhere),
        out_specs=[pl.BlockSpec(memory_space=pltpu.HBM) if to_hbm else in_vmem] * len(outs) + [in_smem] * flag,
        scratch_shapes=scratch,
        compiler_params=pltpu.CompilerParams(vmem_limit_bytes=VMEM_BYTES),
        cost_estimate=pl.CostEstimate(flops=0, bytes_accessed=0, transcendentals=0),
    )(*smem, *vmem, *anywhere)


def body(
    amplitudes, driver, integrals, pair_energy, col_energy, tile_irrep, pair_irrep, mirror_slot
):
    places, sides = lax.axis_size("virt"), lax.axis_size("pair")
    partner_bit = sides.bit_length() - 2
    rows, half_cols = amplitudes.shape
    slab_tiles = integrals.shape[1] // TILE
    plans = [
        Plan(2 * half_cols // TILE, slab_tiles, places, per_tile * slab_tiles)
        for per_tile in CAPS
    ]
    plan = plans[-1]
    z, sub = lax.axis_index("virt"), lax.axis_index("sub")
    side = (lax.axis_index("pair") >> partner_bit) & 1
    place = jnp.stack([z, side, sub]).astype(jnp.int32)

    def like(shape, dtype=integrals.dtype):
        return jax.ShapeDtypeStruct(shape, dtype)

    other_irrep = from_partner(tile_irrep, "sub", 0)
    their_ints = from_partner(integrals, "sub", 0)

    label_row, slot_row, energy_row = pair_irrep[None, :], mirror_slot[None, :], pair_energy[None, :]
    shape = Rows(rows, half_cols)
    sort_scratch = [pltpu.VMEM((shape.sorted, half_cols), amplitudes.dtype)] * 2 + [
        pltpu.SMEM((2 * IRREPS,), jnp.int32),
        pltpu.SMEM((shape.tiles * shape.most + 1,), jnp.int32),
    ]
    bundle, rows_full = call(
        functools.partial(rows_kernel, shape),
        (tile_irrep,),
        (amplitudes, driver, label_row, energy_row),
        [like((shape.sent, TILE))],
        sort_scratch,
        flag=True,
    )

    lists = [pltpu.SMEM((plan.tiles,), jnp.int32), pltpu.SMEM((plan.slab * plan.tiles + 1,), jnp.int32)]
    level, spots = list_tiles_of(plans, lists, tile_irrep, other_irrep, place, bundle)

    def sparse(index):
        return sparse_plan(
            plans[index], spots, place, lists, shape, sort_scratch,
            other_irrep, their_ints, bundle, rows_full, amplitudes, driver, integrals, label_row,
            slot_row, energy_row, col_energy, tile_irrep,
        )

    def dense():
        return dense_plan(
            amplitudes, driver, integrals, pair_energy, col_energy, tile_irrep, pair_irrep,
            mirror_slot,
        )

    branches = [functools.partial(sparse, index) for index in range(len(plans))] + [dense]
    return lax.switch(level[0], branches)


def list_tiles_of(plans, lists, own, other, place, after):
    smem = pl.BlockSpec(memory_space=pltpu.SMEM)

    def kernel(own, other, place, after_ref, *refs):
        list_kernel(plans, own, other, place, *refs)

    return pl.pallas_call(
        kernel,
        out_shape=[
            jax.ShapeDtypeStruct((1,), jnp.int32),
            jax.ShapeDtypeStruct((plans[-1].cap,), jnp.int32),
        ],
        in_specs=[smem] * 3 + [pl.BlockSpec(memory_space=pl.ANY)],
        out_specs=[smem] * 2,
        scratch_shapes=lists + [pltpu.SMEM((plans[-1].tiles,), jnp.int32)],
    )(own, other, place, after)


def sparse_plan(
    plan, spots, place, lists, shape, sort_scratch, other_irrep, their_ints, bundle, rows_full,
    amplitudes, driver, integrals, label_row, slot_row, energy_row, col_energy, tile_irrep,
):
    places, sides = lax.axis_size("virt"), lax.axis_size("pair")
    partner_bit = sides.bit_length() - 2
    rows, half_cols = amplitudes.shape

    def like(shape, dtype=integrals.dtype):
        return jax.ShapeDtypeStruct(shape, dtype)

    def over_pair(value):
        return from_partner(value, "pair", partner_bit)

    sends = call(
        functools.partial(pack_kernel, plan),
        (spots, place),
        (integrals, their_ints),
        [like((plan.part * TILE, TILE))] * 2,
    )

    near = plan.near
    got = []
    for turn in range(max(2 * (near - 1), near)):
        pairs = []
        for i in range(places):
            half, at = i // near, i % near
            if turn < 2 * (near - 1):
                to = half * near + (at + turn // 2 + 1) % near
                pairs.append((2 * i + half, 2 * to + half))
            if turn < near:
                to = (1 - half) * near + (at + turn) % near
                pairs.append((2 * i + 1 - half, 2 * to + half))
        got.append(lax.ppermute(sends[turn % 2], ("virt", "sub"), pairs))
    across = []
    for i in range(places):
        for j in range(sides):
            far = 1 - i // near
            across.append(((i * sides + j) * 2 + far, (i * sides + (j ^ 1 << partner_bit)) * 2 + far))
    near_got, far_got = got, got[:near]
    swapped = [lax.ppermute(value, ("virt", "pair", "sub"), across) for value in far_got]

    other_bundle = over_pair(bundle)
    energy = col_energy[None, :]

    def mirror(whole, more=()):
        return tuple(call(
            functools.partial(mirror_kernel, shape, plan.pieces(2 * rows), whole),
            (tile_irrep,),
            (amplitudes, other_bundle, slot_row, label_row, energy_row, *more),
            [like((2 * rows, tiles * TILE)) for tiles in plan.pieces(2 * rows)]
            + [like((rows, half_cols)), like((3 * rows, TILE), jnp.float32)],
            () if whole else sort_scratch,
        ))

    *cur_mine, mirror_driver, columns = lax.cond(
        rows_full[0] > 0,
        lambda: mirror(True, (over_pair(amplitudes), over_pair(driver))),
        lambda: mirror(False),
    )
    cur_their = [from_partner(piece, "sub", 0) for piece in cur_mine]

    width = plan.slab * TILE
    near_cols, flops = (near - 1) * width, 2 * 2 * rows * plan.tiles * TILE * width
    common = (*cur_mine, *cur_their, driver, mirror_driver, columns, energy)

    def came(turns):
        near_turns, far_turns = turns
        values = [near_got[t] for t in near_turns] + [far_got[t] for t in far_turns]
        return values + [swapped[t] for t in far_turns]

    turns = turns_for(plan, range(near - 1))
    ints_a, a_mine = call(
        functools.partial(early_kernel, plan, turns),
        (tile_irrep, other_irrep, place),
        (integrals, their_ints, *common, *came(turns)),
        [like((plan.tiles * TILE, near_cols)), like((2 * rows, near_cols))],
        lists,
        flops=flops * (near - 1),
    )
    a_their = from_partner(a_mine, "sub", 0)
    (early,) = call(
        functools.partial(early_part_kernel, plan),
        (place,),
        (a_mine, a_their, ints_a),
        [like((rows, near_cols), jnp.float32)],
        flops=flops // 2,
    )
    turns = turns_for(plan, range(near - 1, near))
    ints_b, b_mine = call(
        functools.partial(late_kernel, plan, turns),
        (tile_irrep, other_irrep, place),
        (*common, *came(turns)),
        [like((plan.tiles * TILE, width)), like((2 * rows, width))],
        lists,
        flops=flops,
    )
    b_their = from_partner(b_mine, "sub", 0)
    (sym,) = call(
        functools.partial(part_kernel, plan),
        (place,),
        (a_mine, a_their, b_mine, ints_a, ints_b, early),
        [like((rows, half_cols), jnp.float32)],
        flops=flops,
    )
    return call(
        functools.partial(last_kernel, plan),
        (tile_irrep, place),
        (b_their, ints_a, ints_b, sym, driver, columns, energy),
        [like((rows, half_cols), jnp.float32)],
        [pltpu.VMEM((rows, half_cols), jnp.float32),
         pltpu.SemaphoreType.DMA((len(blocks(plan, near)),))],
        flops=flops // 2,
        to_hbm=True,
    )[0]


def solution(mesh):
    return jax.shard_map(
        body,
        mesh=mesh,
        in_specs=(
            P(("groups", "pair", "virt"), "sub"),
            P(("groups", "pair", "virt"), "sub"),
            P(("groups", "sub"), "virt"),
            P(("groups", "pair", "virt")),
            P(("groups", "sub")),
            P(("groups", "sub")),
            P(("groups", "pair", "virt")),
            P(("groups", "pair", "virt")),
        ),
        out_specs=P(("groups", "pair", "virt"), "sub"),
        check_vma=False,
    )
```

```python
import functools

import jax
import jax.numpy as jnp
from jax import lax
from jax.experimental import pallas as pl
from jax.experimental.pallas import tpu as pltpu
from jax.sharding import PartitionSpec as P

ITERS = 2
TILE = 128
IRREPS = 4
PIECES = 2
CHUNK = 16
CAPS = (5, 6, 7, 8)
VMEM_BYTES = 20 * 1024 * 1024


def from_partner(value, axis, apart):
    return lax.ppermute(value, axis, [(i, i ^ 1 << apart) for i in range(lax.axis_size(axis))])


def contract(blocks, integrals):
    places, z, sub = lax.axis_size("virt"), lax.axis_index("virt"), lax.axis_index("sub")
    width = integrals.shape[1]
    whole = jnp.zeros((integrals.shape[0], places * width), integrals.dtype)
    for apart in range(places):
        slab = integrals
        if apart:
            slab = lax.ppermute(
                integrals, "virt", [(i, (i + apart) % places) for i in range(places)]
            )
        at = lax.rem(z - apart + places, places) * width
        whole = lax.dynamic_update_slice(whole, slab, (0, at))
    total = jnp.dot(blocks[0], whole, preferred_element_type=jnp.float32)
    half = total.shape[1] // 2
    mine = lax.dynamic_slice_in_dim(total, sub * half, half, 1)
    theirs = lax.dynamic_slice_in_dim(total, (1 - sub) * half, half, 1)
    return mine + from_partner(theirs, "sub", 0)


def dense_plan(
    amplitudes, driver, integrals, pair_energy, col_energy, tile_irrep, pair_irrep, mirror_slot
):
    col_irrep = jnp.repeat(tile_irrep, TILE)
    occupied = pair_irrep[:, None] == col_irrep[None, :]
    energy_gap = col_energy[None, :] - pair_energy[:, None]
    driver_wide = driver.astype(jnp.float32)
    partner_bit = lax.axis_size("pair").bit_length() - 2
    current = jnp.where(occupied, amplitudes, jnp.zeros((), amplitudes.dtype))
    updated = driver_wide
    for iteration in range(ITERS):
        ladder = contract((current,), integrals)
        mirror_block = from_partner(ladder, "pair", partner_bit)
        symmetric = ladder + jnp.take(mirror_block, mirror_slot, axis=0)
        updated = jnp.where(
            occupied, (driver_wide + symmetric) / energy_gap, jnp.zeros((), jnp.float32)
        )
        current = updated.astype(jnp.bfloat16)
    return updated


class Plan:
    def __init__(self, tiles, slab_tiles, places, cap):
        self.tiles = tiles
        self.half = tiles // 2
        self.slab = slab_tiles
        self.places = places
        self.near = places // 2
        self.part = -(-cap // 2)
        self.cap = 2 * self.part

    def pieces(self, rows):
        first = max(self.half // 2, self.part * TILE // rows + 1)
        return (first, self.half - first)


def split(value, size):
    assert size & (size - 1) == 0
    return value >> (size.bit_length() - 1), value & (size - 1)


def tile_at(index):
    return pl.ds(pl.multiple_of(index * TILE, TILE), TILE)


def all_labels(plan, own, other, sub, labels):
    for i in range(plan.half):
        labels[sub * plan.half + i] = own[i]
        labels[(1 - sub) * plan.half + i] = other[i]


def list_tiles(plan, labels, slab, spots):
    for n in range(plan.cap):
        spots[n] = 0
    count = jnp.int32(0)
    for j in range(plan.slab):
        here = labels[slab * plan.slab + j]
        for k in range(plan.tiles):
            spots[count] = j * plan.tiles + k
            count += (labels[k] == here).astype(jnp.int32)
    spots[count] = 0


def list_kernel(plans, own, other, place, level_ref, spots_ref, labels, spots, sizes):
    plan = plans[-1]
    all_labels(plan, own, other, place[2], labels)
    for k in range(plan.tiles):
        sizes[k] = 0
    for k in range(plan.tiles):
        sizes[labels[k]] += 1
    most = jnp.int32(0)
    for i in range(plan.places):
        needed = jnp.int32(0)
        for j in range(plan.slab):
            needed += sizes[labels[i * plan.slab + j]]
        most = jnp.maximum(most, needed)
    level = jnp.int32(0)
    for each in plans:
        level += (most > each.cap).astype(jnp.int32)
    level_ref[0] = level
    list_tiles(plan, labels, place[0], spots)
    for n in range(plan.cap):
        spots_ref[n] = spots[n]


def pack_kernel(plan, spots, place, mine_ref, their_ref, *send_refs):
    slab, side, sub = place[0], place[1], place[2]
    is_near = slab // plan.near == sub
    for i, to_ref in enumerate(send_refs):
        first = jnp.where(is_near, i, side) * plan.part
        for n in range(plan.part):
            spot = spots[first + n]
            j, k = split(spot, plan.tiles)
            core, row = split(k, plan.half)
            rows, cols = tile_at(row), tile_at(j)
            to_ref[n * TILE : (n + 1) * TILE, :] = jnp.where(
                core == sub, mine_ref[rows, cols], their_ref[rows, cols]
            )


def column(row):
    n = row.shape[1]
    here = lax.broadcasted_iota(jnp.int32, (n, n), 0) == lax.broadcasted_iota(jnp.int32, (n, n), 1)
    return jnp.sum(jnp.where(here, row.astype(jnp.float32), 0.0), axis=1, keepdims=True)


def mirror_table(slot_row):
    n = slot_row.shape[1]
    slots = column(slot_row).astype(jnp.int32)
    return lax.broadcasted_iota(jnp.int32, (n, n), 1) == slots


class Rows:
    def __init__(self, rows, cols):
        self.rows = rows
        self.sorted = rows + IRREPS * CHUNK
        self.tiles = cols // TILE
        self.most = -(-rows // CHUNK)
        self.cap = self.tiles * self.most * 2 // 5
        self.energy = -(-rows // TILE)
        self.sent = (2 * self.cap + self.energy) * CHUNK


def list_chunks(shape, own, label_row, sizes, spots):
    firsts, first = [], jnp.int32(0)
    for g in range(IRREPS):
        count = jnp.sum(jnp.where(label_row == g, 1.0, 0.0)).astype(jnp.int32)
        chunks = (count + CHUNK - 1) // CHUNK
        sizes[g], sizes[IRREPS + g] = first, chunks
        firsts.append(first * CHUNK)
        first += chunks
    for n in range(shape.cap):
        spots[n] = 0
    total = jnp.int32(0)
    for j in range(shape.tiles):
        first, chunks = sizes[own[j]], sizes[IRREPS + own[j]]
        for c in range(shape.most):
            spots[total] = j * TILE + first + c
            total += (c < chunks).astype(jnp.int32)
    spots[total] = 0
    return total, firsts


def first_of(labels, firsts):
    value = jnp.zeros(labels.shape, jnp.float32)
    for g, first in enumerate(firsts):
        value = jnp.where(labels == g, first.astype(jnp.float32), value)
    return value


def chunk_at(spot):
    j, chunk = split(spot, TILE)
    return pl.ds(pl.multiple_of(chunk * CHUNK, CHUNK), CHUNK), tile_at(j)


def rows_kernel(
    shape, own, amps_ref, driver_ref, label_row, energy_row, out_ref, full_ref, amps, drivers, sizes,
    spots,
):
    n = shape.rows
    total, firsts = list_chunks(shape, own, label_row[...], sizes, spots)
    full_ref[0] = (total > shape.cap).astype(jnp.int32)
    labels = column(label_row[...]).astype(jnp.int32)
    above = lax.broadcasted_iota(jnp.int32, (n, n), 0) < lax.broadcasted_iota(jnp.int32, (n, n), 1)
    rank = jnp.where((labels == label_row[...]) & above, 1.0, 0.0).sum(axis=0, keepdims=True)
    spot_row = (rank + first_of(label_row[...], firsts)).astype(jnp.int32)
    order = lax.broadcasted_iota(jnp.int32, (shape.sorted, n), 0) == spot_row
    order = order.astype(jnp.bfloat16)
    for to_ref, from_ref in ((amps, amps_ref), (drivers, driver_ref)):
        to_ref[...] = jnp.dot(order, from_ref[...], preferred_element_type=jnp.float32).astype(
            to_ref.dtype
        )
    for i in range(shape.cap):
        rows, cols = chunk_at(spots[i])
        out_ref[i * CHUNK : (i + 1) * CHUNK, :] = amps[rows, cols]
        out_ref[(shape.cap + i) * CHUNK : (shape.cap + i + 1) * CHUNK, :] = drivers[rows, cols]

    rest = jnp.broadcast_to(energy_row[...], (CHUNK, n))
    at = lax.broadcasted_iota(jnp.int32, (CHUNK, n), 0)
    terms = jnp.zeros((CHUNK, n), jnp.float32)
    for i in range(3):
        term = rest.astype(jnp.bfloat16).astype(jnp.float32)
        terms = jnp.where(at == i, term, terms)
        rest = rest - term
    for i in range(shape.energy):
        width = min(TILE, n - i * TILE)
        first = (2 * shape.cap + i) * CHUNK
        out_ref[first : first + CHUNK, :] = jnp.zeros((CHUNK, TILE), out_ref.dtype)
        out_ref[first : first + CHUNK, :width] = terms[:, i * TILE : i * TILE + width].astype(
            out_ref.dtype
        )


def mirror_kernel(shape, pieces, whole, own, amps_ref, bundle_ref, slot_row, label_row, energy_row, *refs):
    if whole:
        amps, drivers, *cur_refs, mirror_driver_ref, columns_ref = refs
    else:
        *cur_refs, mirror_driver_ref, columns_ref, amps, drivers, sizes, spots = refs
    rows = shape.rows
    table = mirror_table(slot_row[...])
    row_label = column(label_row[...])
    if whole:
        weights = table
    else:
        total, firsts = list_chunks(shape, own, label_row[...], sizes, spots)
        amps[...] = jnp.zeros_like(amps)
        drivers[...] = jnp.zeros_like(drivers)
        for i in range(shape.cap):
            at = chunk_at(spots[i])
            amps[at] = bundle_ref[i * CHUNK : (i + 1) * CHUNK, :]
            drivers[at] = bundle_ref[(shape.cap + i) * CHUNK : (shape.cap + i + 1) * CHUNK, :]
        slots = column(slot_row[...]).astype(jnp.int32)
        before = (row_label == label_row[...].astype(jnp.float32)) & (slot_row[...] < slots)
        rank = jnp.where(before, 1.0, 0.0).sum(axis=1, keepdims=True)
        spot = (rank + first_of(row_label, firsts)).astype(jnp.int32)
        weights = lax.broadcasted_iota(jnp.int32, (rows, shape.sorted), 1) == spot
    weights = weights.astype(jnp.bfloat16)
    mirrored = jnp.dot(weights, amps[...], preferred_element_type=jnp.float32)
    zero = jnp.zeros((), amps_ref.dtype)
    for j in range(shape.tiles):
        cols = slice(j * TILE, (j + 1) * TILE)
        cur_ref, first = (cur_refs[0], 0) if j < pieces[0] else (cur_refs[1], pieces[0])
        at = slice((j - first) * TILE, (j - first + 1) * TILE)
        occupied = row_label == own[j].astype(jnp.float32)
        cur_ref[:rows, at] = jnp.where(occupied, amps_ref[:, cols], zero)
        cur_ref[rows:, at] = jnp.where(occupied, mirrored[:, cols], 0.0).astype(cur_ref.dtype)
    mirror_driver_ref[...] = jnp.dot(
        weights, drivers[...], preferred_element_type=jnp.float32
    ).astype(mirror_driver_ref.dtype)
    mirror_energy = jnp.zeros((rows, 1), jnp.float32)
    for i in range(shape.energy):
        width = min(TILE, rows - i * TILE)
        first = (2 * shape.cap + i) * CHUNK
        terms = bundle_ref[first : first + CHUNK, :width].astype(jnp.float32)
        other_energy = (terms[0:1] + terms[1:2]) + terms[2:3]
        here = table[:, i * TILE : i * TILE + width]
        mirror_energy += jnp.where(here, other_energy, 0.0).sum(axis=1, keepdims=True)
    for i, value in enumerate((row_label, column(energy_row[...]), mirror_energy)):
        columns_ref[i * rows : (i + 1) * rows, :] = jnp.broadcast_to(value, (rows, TILE))


def bounds(plan, core, first, count):
    return pl.ds(pl.multiple_of(core * plan.half * TILE + first, TILE), count)


def first_column(plan, place, i):
    here = lax.rem(place[0], plan.near)
    return lax.rem(here + 2 + i, plan.near) * plan.slab * TILE


def slot_of_near(plan, turn):
    return (-(turn // 2 + 1) - 2) % plan.near


def slot_of_far(plan, turn):
    return (-turn - 2) % plan.near


def turns_for(plan, slots):
    return (
        [t for t in range(2 * (plan.near - 1)) if slot_of_near(plan, t) in slots],
        [t for t in range(plan.near) if slot_of_far(plan, t) in slots],
    )


def fill(plan, slots, own, other, place, near_got, far_got, swapped, ints_ref, labels, spots):
    z, side, sub = place[0], place[1], place[2]
    here = lax.rem(z, plan.near)
    ints_ref[...] = jnp.zeros_like(ints_ref)
    all_labels(plan, own, other, sub, labels)
    near_turns, far_turns = turns_for(plan, slots)

    def put(slot, n, value):
        spot = spots[n]
        j, k = split(spot, plan.tiles)
        ints_ref[tile_at(k), tile_at((slot - slots[0]) * plan.slab + j)] = value

    def list_slot(slot):
        slab = sub * plan.near + lax.rem(here + 2 + slot, plan.near)
        list_tiles(plan, labels, slab, spots)

    @pl.when(z // plan.near == sub)
    def _():
        for turn in near_turns:
            slot = slot_of_near(plan, turn)
            if turn % 2 == 0:
                list_slot(slot)
            for n in range(plan.part):
                tile = near_got[turn][n * TILE : (n + 1) * TILE, :]
                put(slot, turn % 2 * plan.part + n, tile)

    @pl.when(z // plan.near != sub)
    def _():
        for turn in far_turns:
            slot = slot_of_far(plan, turn)
            list_slot(slot)
            for n in range(plan.part):
                rows = slice(n * TILE, (n + 1) * TILE)
                put(slot, side * plan.part + n, far_got[turn][rows, :])
                put(slot, (1 - side) * plan.part + n, swapped[turn][rows, :])


def new_current(plan, slots, own, place, pieces, ints_ref, driver, mirror_driver, columns, col_energy,
                cur_ref):
    rows = driver.shape[0]
    width = plan.slab * TILE
    wide = min(width, 2 * TILE)
    terms = []
    for i, piece in enumerate(pieces):
        core = place[2] if i < PIECES else 1 - place[2]
        sizes = [tiles * TILE for tiles in plan.pieces(2 * rows)]
        terms.append((piece, bounds(plan, core, i % PIECES * sizes[0], sizes[i % PIECES])))
    for slot in slots:
        first = first_column(plan, place, slot)
        for c in range(0, width, wide):
            cols = slice((slot - slots[0]) * width + c, (slot - slots[0]) * width + c + wide)
            total = None
            for piece, at in terms:
                term = jnp.dot(piece[...], ints_ref[at, cols], preferred_element_type=jnp.float32)
                total = term if total is None else total + term
            sym = total[:rows] + total[rows:]
            for t in range(0, wide, TILE):
                at = pl.ds(pl.multiple_of(first + c + t, TILE), TILE)
                occupied = columns[:rows] == own[(first + c + t) // TILE].astype(jnp.float32)
                for i, source in enumerate((driver, mirror_driver)):
                    gap = col_energy[:, at] - columns[(i + 1) * rows : (i + 2) * rows]
                    new = (source[:, at].astype(jnp.float32) + sym[:, t : t + TILE]) / gap
                    new = jnp.where(occupied, new, 0.0)
                    cur_ref[i * rows : (i + 1) * rows, cols.start + t : cols.start + t + TILE] = (
                        new.astype(cur_ref.dtype)
                    )


def take_turns(turns, refs):
    refs = list(refs)
    return [{t: refs.pop(0) for t in each} for each in (turns[0], turns[1], turns[1])]


def early_kernel(plan, turns, *refs):
    own, other, place, mine_ref, their_ref = refs[:5]
    pieces, refs = refs[5 : 5 + 2 * PIECES], refs[5 + 2 * PIECES :]
    came = take_turns(turns, refs[4:-4])
    ints_ref, cur_ref, labels, spots = refs[-4:]
    slots = range(plan.near - 1)
    width = plan.slab * TILE
    fill(plan, slots, own, other, place, *came, ints_ref, labels, spots)

    @pl.when(place[0] // plan.near == place[2])
    def _():
        cols = slice((plan.near - 2) * width, (plan.near - 1) * width)
        ints_ref[bounds(plan, place[2], 0, plan.half * TILE), cols] = mine_ref[...]
        ints_ref[bounds(plan, 1 - place[2], 0, plan.half * TILE), cols] = their_ref[...]

    new_current(plan, slots, own, place, pieces, ints_ref, *refs[:4], cur_ref)


def late_kernel(plan, turns, *refs):
    own, other, place = refs[:3]
    pieces, refs = refs[3 : 3 + 2 * PIECES], refs[3 + 2 * PIECES :]
    came = take_turns(turns, refs[4:-4])
    ints_ref, cur_ref, labels, spots = refs[-4:]
    slots = range(plan.near - 1, plan.near)
    fill(plan, slots, own, other, place, *came, ints_ref, labels, spots)
    new_current(plan, slots, own, place, pieces, ints_ref, *refs[:4], cur_ref)


def product(plan, place, terms, ints_ref, cols):
    width = plan.slab * TILE
    total = None
    for cur_ref, core, slots in terms:
        for slot in slots:
            at = slice((slot - slots[0]) * width, (slot - slots[0] + 1) * width)
            rows = bounds(plan, core, first_column(plan, place, slot), width)
            term = jnp.dot(
                cur_ref[:, at], ints_ref[rows, cols], preferred_element_type=jnp.float32
            )
            total = term if total is None else total + term
    half = total.shape[0] // 2
    return total[:half] + total[half:]


def blocks(plan, count):
    width = plan.slab * TILE
    wide = min(width, 2 * TILE)
    return [slice(c, c + wide) for c in range(0, count * width, wide)]


def early_part_kernel(plan, place, a_mine, a_their, ints_a, sym_ref):
    a = range(plan.near - 1)
    terms = [(a_mine, place[2], a), (a_their, 1 - place[2], a)]
    for cols in blocks(plan, plan.near - 1):
        sym_ref[:, cols] = product(plan, place, terms, ints_a, cols)


def part_kernel(plan, place, a_mine, a_their, b_mine, ints_a, ints_b, early_ref, sym_ref):
    a, b = range(plan.near - 1), range(plan.near - 1, plan.near)
    terms = [(b_mine, place[2], b)]
    for cols in blocks(plan, plan.near - 1):
        sym_ref[:, cols] = early_ref[:, cols] + product(plan, place, terms, ints_a, cols)
    terms = [(a_mine, place[2], a), (a_their, 1 - place[2], a), (b_mine, place[2], b)]
    width = (plan.near - 1) * plan.slab * TILE
    for cols in blocks(plan, 1):
        sym_ref[:, width + cols.start : width + cols.stop] = product(plan, place, terms, ints_b, cols)


def last_kernel(plan, own, place, b_their, ints_a, ints_b, sym_ref, driver, columns, col_energy, out_ref,
                new_ref, sems):
    rows = driver.shape[0]
    terms = [(b_their, 1 - place[2], range(plan.near - 1, plan.near))]
    width = plan.slab * TILE
    copies = []
    for c, cols in enumerate(blocks(plan, plan.near)):
        slot = cols.start // width
        ints_ref, start = (ints_b, cols.start - slot * width) if slot == plan.near - 1 else (ints_a, cols.start)
        wide = cols.stop - cols.start
        sym = sym_ref[:, cols] + product(plan, place, terms, ints_ref, slice(start, start + wide))
        first = first_column(plan, place, slot) + cols.start - slot * width
        for t in range(0, wide, TILE):
            at = pl.ds(pl.multiple_of(first + t, TILE), TILE)
            occupied = columns[:rows] == own[(first + t) // TILE].astype(jnp.float32)
            gap = col_energy[:, at] - columns[rows : 2 * rows]
            new = (driver[:, at].astype(jnp.float32) + sym[:, t : t + TILE]) / gap
            new_ref[:, cols.start + t : cols.start + t + TILE] = jnp.where(occupied, new, 0.0)
        at = pl.ds(pl.multiple_of(first, TILE), wide)
        copy = pltpu.make_async_copy(new_ref.at[:, cols], out_ref.at[:, at], sems.at[c])
        copy.start()
        copies.append(copy)
    for copy in copies:
        copy.wait()


def call(kernel, smem, vmem, outs, scratch=(), anywhere=(), flag=False, flops=0, to_hbm=False):
    moved = sum(v.size * v.dtype.itemsize for v in vmem)
    in_smem, in_vmem = pl.BlockSpec(memory_space=pltpu.SMEM), pl.BlockSpec(memory_space=pltpu.VMEM)
    in_any = pl.BlockSpec(memory_space=pl.ANY)
    return pl.pallas_call(
        kernel,
        out_shape=list(outs) + [jax.ShapeDtypeStruct((1,), jnp.int32)] * flag,
        in_specs=[in_smem] * len(smem) + [in_vmem] * len(vmem) + [in_any] * len(anywhere),
        out_specs=[pl.BlockSpec(memory_space=pltpu.HBM) if to_hbm else in_vmem] * len(outs) + [in_smem] * flag,
        scratch_shapes=scratch,
        compiler_params=pltpu.CompilerParams(vmem_limit_bytes=VMEM_BYTES),
        cost_estimate=pl.CostEstimate(flops=0, bytes_accessed=0, transcendentals=0),
    )(*smem, *vmem, *anywhere)


def body(
    amplitudes, driver, integrals, pair_energy, col_energy, tile_irrep, pair_irrep, mirror_slot
):
    places, sides = lax.axis_size("virt"), lax.axis_size("pair")
    partner_bit = sides.bit_length() - 2
    rows, half_cols = amplitudes.shape
    slab_tiles = integrals.shape[1] // TILE
    plans = [
        Plan(2 * half_cols // TILE, slab_tiles, places, per_tile * slab_tiles)
        for per_tile in CAPS
    ]
    plan = plans[-1]
    z, sub = lax.axis_index("virt"), lax.axis_index("sub")
    side = (lax.axis_index("pair") >> partner_bit) & 1
    place = jnp.stack([z, side, sub]).astype(jnp.int32)

    def like(shape, dtype=integrals.dtype):
        return jax.ShapeDtypeStruct(shape, dtype)

    other_irrep = from_partner(tile_irrep, "sub", 0)
    their_ints = from_partner(integrals, "sub", 0)

    label_row, slot_row, energy_row = pair_irrep[None, :], mirror_slot[None, :], pair_energy[None, :]
    shape = Rows(rows, half_cols)
    sort_scratch = [pltpu.VMEM((shape.sorted, half_cols), amplitudes.dtype)] * 2 + [
        pltpu.SMEM((2 * IRREPS,), jnp.int32),
        pltpu.SMEM((shape.tiles * shape.most + 1,), jnp.int32),
    ]
    bundle, rows_full = call(
        functools.partial(rows_kernel, shape),
        (tile_irrep,),
        (amplitudes, driver, label_row, energy_row),
        [like((shape.sent, TILE))],
        sort_scratch,
        flag=True,
    )

    lists = [pltpu.SMEM((plan.tiles,), jnp.int32), pltpu.SMEM((plan.slab * plan.tiles + 1,), jnp.int32)]
    level, spots = list_tiles_of(plans, lists, tile_irrep, other_irrep, place, bundle)

    def sparse(index):
        return sparse_plan(
            plans[index], spots, place, lists, shape, sort_scratch,
            other_irrep, their_ints, bundle, rows_full, amplitudes, driver, integrals, label_row,
            slot_row, energy_row, col_energy, tile_irrep,
        )

    def dense():
        return dense_plan(
            amplitudes, driver, integrals, pair_energy, col_energy, tile_irrep, pair_irrep,
            mirror_slot,
        )

    branches = [functools.partial(sparse, index) for index in range(len(plans))] + [dense]
    return lax.switch(level[0], branches)


def list_tiles_of(plans, lists, own, other, place, after):
    smem = pl.BlockSpec(memory_space=pltpu.SMEM)

    def kernel(own, other, place, after_ref, *refs):
        list_kernel(plans, own, other, place, *refs)

    return pl.pallas_call(
        kernel,
        out_shape=[
            jax.ShapeDtypeStruct((1,), jnp.int32),
            jax.ShapeDtypeStruct((plans[-1].cap,), jnp.int32),
        ],
        in_specs=[smem] * 3 + [pl.BlockSpec(memory_space=pl.ANY)],
        out_specs=[smem] * 2,
        scratch_shapes=lists + [pltpu.SMEM((plans[-1].tiles,), jnp.int32)],
    )(own, other, place, after)


def sparse_plan(
    plan, spots, place, lists, shape, sort_scratch, other_irrep, their_ints, bundle, rows_full,
    amplitudes, driver, integrals, label_row, slot_row, energy_row, col_energy, tile_irrep,
):
    places, sides = lax.axis_size("virt"), lax.axis_size("pair")
    partner_bit = sides.bit_length() - 2
    rows, half_cols = amplitudes.shape

    def like(shape, dtype=integrals.dtype):
        return jax.ShapeDtypeStruct(shape, dtype)

    def over_pair(value):
        return from_partner(value, "pair", partner_bit)

    sends = call(
        functools.partial(pack_kernel, plan),
        (spots, place),
        (integrals, their_ints),
        [like((plan.part * TILE, TILE))] * 2,
    )

    near = plan.near
    got = []
    for turn in range(max(2 * (near - 1), near)):
        pairs = []
        for i in range(places):
            half, at = i // near, i % near
            if turn < 2 * (near - 1):
                to = half * near + (at + turn // 2 + 1) % near
                pairs.append((2 * i + half, 2 * to + half))
            if turn < near:
                to = (1 - half) * near + (at + turn) % near
                pairs.append((2 * i + 1 - half, 2 * to + half))
        got.append(lax.ppermute(sends[turn % 2], ("virt", "sub"), pairs))
    across = []
    for i in range(places):
        for j in range(sides):
            far = 1 - i // near
            across.append(((i * sides + j) * 2 + far, (i * sides + (j ^ 1 << partner_bit)) * 2 + far))
    near_got, far_got = got, got[:near]
    swapped = [lax.ppermute(value, ("virt", "pair", "sub"), across) for value in far_got]

    other_bundle = over_pair(bundle)
    energy = col_energy[None, :]

    def mirror(whole, more=()):
        return tuple(call(
            functools.partial(mirror_kernel, shape, plan.pieces(2 * rows), whole),
            (tile_irrep,),
            (amplitudes, other_bundle, slot_row, label_row, energy_row, *more),
            [like((2 * rows, tiles * TILE)) for tiles in plan.pieces(2 * rows)]
            + [like((rows, half_cols)), like((3 * rows, TILE), jnp.float32)],
            () if whole else sort_scratch,
        ))

    *cur_mine, mirror_driver, columns = lax.cond(
        rows_full[0] > 0,
        lambda: mirror(True, (over_pair(amplitudes), over_pair(driver))),
        lambda: mirror(False),
    )
    cur_their = [from_partner(piece, "sub", 0) for piece in cur_mine]

    width = plan.slab * TILE
    near_cols, flops = (near - 1) * width, 2 * 2 * rows * plan.tiles * TILE * width
    common = (*cur_mine, *cur_their, driver, mirror_driver, columns, energy)

    def came(turns):
        near_turns, far_turns = turns
        values = [near_got[t] for t in near_turns] + [far_got[t] for t in far_turns]
        return values + [swapped[t] for t in far_turns]

    turns = turns_for(plan, range(near - 1))
    ints_a, a_mine = call(
        functools.partial(early_kernel, plan, turns),
        (tile_irrep, other_irrep, place),
        (integrals, their_ints, *common, *came(turns)),
        [like((plan.tiles * TILE, near_cols)), like((2 * rows, near_cols))],
        lists,
        flops=flops * (near - 1),
    )
    a_their = from_partner(a_mine, "sub", 0)
    (early,) = call(
        functools.partial(early_part_kernel, plan),
        (place,),
        (a_mine, a_their, ints_a),
        [like((rows, near_cols), jnp.float32)],
        flops=flops // 2,
    )
    turns = turns_for(plan, range(near - 1, near))
    ints_b, b_mine = call(
        functools.partial(late_kernel, plan, turns),
        (tile_irrep, other_irrep, place),
        (*common, *came(turns)),
        [like((plan.tiles * TILE, width)), like((2 * rows, width))],
        lists,
        flops=flops,
    )
    b_their = from_partner(b_mine, "sub", 0)
    (sym,) = call(
        functools.partial(part_kernel, plan),
        (place,),
        (a_mine, a_their, b_mine, ints_a, ints_b, early),
        [like((rows, half_cols), jnp.float32)],
        flops=flops,
    )
    return call(
        functools.partial(last_kernel, plan),
        (tile_irrep, place),
        (b_their, ints_a, ints_b, sym, driver, columns, energy),
        [like((rows, half_cols), jnp.float32)],
        [pltpu.VMEM((rows, half_cols), jnp.float32),
         pltpu.SemaphoreType.DMA((len(blocks(plan, near)),))],
        flops=flops // 2,
        to_hbm=True,
    )[0]


def solution(mesh):
    return jax.shard_map(
        body,
        mesh=mesh,
        in_specs=(
            P(("groups", "pair", "virt"), "sub"),
            P(("groups", "pair", "virt"), "sub"),
            P(("groups", "sub"), "virt"),
            P(("groups", "pair", "virt")),
            P(("groups", "sub")),
            P(("groups", "sub")),
            P(("groups", "pair", "virt")),
            P(("groups", "pair", "virt")),
        ),
        out_specs=P(("groups", "pair", "virt"), "sub"),
        check_vma=False,
    )
```

```python
import functools

import jax
import jax.numpy as jnp
from jax import lax
from jax.experimental import pallas as pl
from jax.experimental.pallas import tpu as pltpu
from jax.sharding import PartitionSpec as P

ITERS = 2
TILE = 128
IRREPS = 4
PIECES = 2
CHUNK = 16
CAPS = (5, 6, 7, 9)
VMEM_BYTES = 20 * 1024 * 1024


def from_partner(value, axis, apart):
    return lax.ppermute(value, axis, [(i, i ^ 1 << apart) for i in range(lax.axis_size(axis))])


def contract(blocks, integrals):
    places, z, sub = lax.axis_size("virt"), lax.axis_index("virt"), lax.axis_index("sub")
    width = integrals.shape[1]
    whole = jnp.zeros((integrals.shape[0], places * width), integrals.dtype)
    for apart in range(places):
        slab = integrals
        if apart:
            slab = lax.ppermute(
                integrals, "virt", [(i, (i + apart) % places) for i in range(places)]
            )
        at = lax.rem(z - apart + places, places) * width
        whole = lax.dynamic_update_slice(whole, slab, (0, at))
    total = jnp.dot(blocks[0], whole, preferred_element_type=jnp.float32)
    half = total.shape[1] // 2
    mine = lax.dynamic_slice_in_dim(total, sub * half, half, 1)
    theirs = lax.dynamic_slice_in_dim(total, (1 - sub) * half, half, 1)
    return mine + from_partner(theirs, "sub", 0)


def dense_plan(
    amplitudes, driver, integrals, pair_energy, col_energy, tile_irrep, pair_irrep, mirror_slot
):
    col_irrep = jnp.repeat(tile_irrep, TILE)
    occupied = pair_irrep[:, None] == col_irrep[None, :]
    energy_gap = col_energy[None, :] - pair_energy[:, None]
    driver_wide = driver.astype(jnp.float32)
    partner_bit = lax.axis_size("pair").bit_length() - 2
    current = jnp.where(occupied, amplitudes, jnp.zeros((), amplitudes.dtype))
    updated = driver_wide
    for iteration in range(ITERS):
        ladder = contract((current,), integrals)
        mirror_block = from_partner(ladder, "pair", partner_bit)
        symmetric = ladder + jnp.take(mirror_block, mirror_slot, axis=0)
        updated = jnp.where(
            occupied, (driver_wide + symmetric) / energy_gap, jnp.zeros((), jnp.float32)
        )
        current = updated.astype(jnp.bfloat16)
    return updated


class Plan:
    def __init__(self, tiles, slab_tiles, places, cap):
        self.tiles = tiles
        self.half = tiles // 2
        self.slab = slab_tiles
        self.places = places
        self.near = places // 2
        self.part = -(-cap // 2)
        self.cap = 2 * self.part

    def pieces(self, rows):
        first = max(self.half // 2, self.part * TILE // rows + 1)
        return (first, self.half - first)


def split(value, size):
    assert size & (size - 1) == 0
    return value >> (size.bit_length() - 1), value & (size - 1)


def tile_at(index):
    return pl.ds(pl.multiple_of(index * TILE, TILE), TILE)


def all_labels(plan, own, other, sub, labels):
    for i in range(plan.half):
        labels[sub * plan.half + i] = own[i]
        labels[(1 - sub) * plan.half + i] = other[i]


def list_tiles(plan, labels, slab, spots):
    for n in range(plan.cap):
        spots[n] = 0
    count = jnp.int32(0)
    for j in range(plan.slab):
        here = labels[slab * plan.slab + j]
        for k in range(plan.tiles):
            spots[count] = j * plan.tiles + k
            count += (labels[k] == here).astype(jnp.int32)
    spots[count] = 0


def list_kernel(plans, own, other, place, level_ref, spots_ref, labels, spots, sizes):
    plan = plans[-1]
    all_labels(plan, own, other, place[2], labels)
    for k in range(plan.tiles):
        sizes[k] = 0
    for k in range(plan.tiles):
        sizes[labels[k]] += 1
    most = jnp.int32(0)
    for i in range(plan.places):
        needed = jnp.int32(0)
        for j in range(plan.slab):
            needed += sizes[labels[i * plan.slab + j]]
        most = jnp.maximum(most, needed)
    level = jnp.int32(0)
    for each in plans:
        level += (most > each.cap).astype(jnp.int32)
    level_ref[0] = level
    list_tiles(plan, labels, place[0], spots)
    for n in range(plan.cap):
        spots_ref[n] = spots[n]


def pack_kernel(plan, spots, place, mine_ref, their_ref, *send_refs):
    slab, side, sub = place[0], place[1], place[2]
    is_near = slab // plan.near == sub
    for i, to_ref in enumerate(send_refs):
        first = jnp.where(is_near, i, side) * plan.part
        for n in range(plan.part):
            spot = spots[first + n]
            j, k = split(spot, plan.tiles)
            core, row = split(k, plan.half)
            rows, cols = tile_at(row), tile_at(j)
            to_ref[n * TILE : (n + 1) * TILE, :] = jnp.where(
                core == sub, mine_ref[rows, cols], their_ref[rows, cols]
            )


def column(row):
    n = row.shape[1]
    here = lax.broadcasted_iota(jnp.int32, (n, n), 0) == lax.broadcasted_iota(jnp.int32, (n, n), 1)
    return jnp.sum(jnp.where(here, row.astype(jnp.float32), 0.0), axis=1, keepdims=True)


def mirror_table(slot_row):
    n = slot_row.shape[1]
    slots = column(slot_row).astype(jnp.int32)
    return lax.broadcasted_iota(jnp.int32, (n, n), 1) == slots


class Rows:
    def __init__(self, rows, cols):
        self.rows = rows
        self.sorted = rows + IRREPS * CHUNK
        self.tiles = cols // TILE
        self.most = -(-rows // CHUNK)
        self.cap = self.tiles * self.most * 2 // 5
        self.energy = -(-rows // TILE)
        self.sent = (2 * self.cap + self.energy) * CHUNK


def list_chunks(shape, own, label_row, sizes, spots):
    firsts, first = [], jnp.int32(0)
    for g in range(IRREPS):
        count = jnp.sum(jnp.where(label_row == g, 1.0, 0.0)).astype(jnp.int32)
        chunks = (count + CHUNK - 1) // CHUNK
        sizes[g], sizes[IRREPS + g] = first, chunks
        firsts.append(first * CHUNK)
        first += chunks
    for n in range(shape.cap):
        spots[n] = 0
    total = jnp.int32(0)
    for j in range(shape.tiles):
        first, chunks = sizes[own[j]], sizes[IRREPS + own[j]]
        for c in range(shape.most):
            spots[total] = j * TILE + first + c
            total += (c < chunks).astype(jnp.int32)
    spots[total] = 0
    return total, firsts


def first_of(labels, firsts):
    value = jnp.zeros(labels.shape, jnp.float32)
    for g, first in enumerate(firsts):
        value = jnp.where(labels == g, first.astype(jnp.float32), value)
    return value


def chunk_at(spot):
    j, chunk = split(spot, TILE)
    return pl.ds(pl.multiple_of(chunk * CHUNK, CHUNK), CHUNK), tile_at(j)


def rows_kernel(
    shape, own, amps_ref, driver_ref, label_row, energy_row, out_ref, full_ref, amps, drivers, sizes,
    spots,
):
    n = shape.rows
    total, firsts = list_chunks(shape, own, label_row[...], sizes, spots)
    full_ref[0] = (total > shape.cap).astype(jnp.int32)
    labels = column(label_row[...]).astype(jnp.int32)
    above = lax.broadcasted_iota(jnp.int32, (n, n), 0) < lax.broadcasted_iota(jnp.int32, (n, n), 1)
    rank = jnp.where((labels == label_row[...]) & above, 1.0, 0.0).sum(axis=0, keepdims=True)
    spot_row = (rank + first_of(label_row[...], firsts)).astype(jnp.int32)
    order = lax.broadcasted_iota(jnp.int32, (shape.sorted, n), 0) == spot_row
    order = order.astype(jnp.bfloat16)
    for to_ref, from_ref in ((amps, amps_ref), (drivers, driver_ref)):
        to_ref[...] = jnp.dot(order, from_ref[...], preferred_element_type=jnp.float32).astype(
            to_ref.dtype
        )
    for i in range(shape.cap):
        rows, cols = chunk_at(spots[i])
        out_ref[i * CHUNK : (i + 1) * CHUNK, :] = amps[rows, cols]
        out_ref[(shape.cap + i) * CHUNK : (shape.cap + i + 1) * CHUNK, :] = drivers[rows, cols]

    rest = jnp.broadcast_to(energy_row[...], (CHUNK, n))
    at = lax.broadcasted_iota(jnp.int32, (CHUNK, n), 0)
    terms = jnp.zeros((CHUNK, n), jnp.float32)
    for i in range(3):
        term = rest.astype(jnp.bfloat16).astype(jnp.float32)
        terms = jnp.where(at == i, term, terms)
        rest = rest - term
    for i in range(shape.energy):
        width = min(TILE, n - i * TILE)
        first = (2 * shape.cap + i) * CHUNK
        out_ref[first : first + CHUNK, :] = jnp.zeros((CHUNK, TILE), out_ref.dtype)
        out_ref[first : first + CHUNK, :width] = terms[:, i * TILE : i * TILE + width].astype(
            out_ref.dtype
        )


def mirror_kernel(shape, pieces, whole, own, amps_ref, bundle_ref, slot_row, label_row, energy_row, *refs):
    if whole:
        amps, drivers, *cur_refs, mirror_driver_ref, columns_ref = refs
    else:
        *cur_refs, mirror_driver_ref, columns_ref, amps, drivers, sizes, spots = refs
    rows = shape.rows
    table = mirror_table(slot_row[...])
    row_label = column(label_row[...])
    if whole:
        weights = table
    else:
        total, firsts = list_chunks(shape, own, label_row[...], sizes, spots)
        amps[...] = jnp.zeros_like(amps)
        drivers[...] = jnp.zeros_like(drivers)
        for i in range(shape.cap):
            at = chunk_at(spots[i])
            amps[at] = bundle_ref[i * CHUNK : (i + 1) * CHUNK, :]
            drivers[at] = bundle_ref[(shape.cap + i) * CHUNK : (shape.cap + i + 1) * CHUNK, :]
        slots = column(slot_row[...]).astype(jnp.int32)
        before = (row_label == label_row[...].astype(jnp.float32)) & (slot_row[...] < slots)
        rank = jnp.where(before, 1.0, 0.0).sum(axis=1, keepdims=True)
        spot = (rank + first_of(row_label, firsts)).astype(jnp.int32)
        weights = lax.broadcasted_iota(jnp.int32, (rows, shape.sorted), 1) == spot
    weights = weights.astype(jnp.bfloat16)
    mirrored = jnp.dot(weights, amps[...], preferred_element_type=jnp.float32)
    zero = jnp.zeros((), amps_ref.dtype)
    for j in range(shape.tiles):
        cols = slice(j * TILE, (j + 1) * TILE)
        cur_ref, first = (cur_refs[0], 0) if j < pieces[0] else (cur_refs[1], pieces[0])
        at = slice((j - first) * TILE, (j - first + 1) * TILE)
        occupied = row_label == own[j].astype(jnp.float32)
        cur_ref[:rows, at] = jnp.where(occupied, amps_ref[:, cols], zero)
        cur_ref[rows:, at] = jnp.where(occupied, mirrored[:, cols], 0.0).astype(cur_ref.dtype)
    mirror_driver_ref[...] = jnp.dot(
        weights, drivers[...], preferred_element_type=jnp.float32
    ).astype(mirror_driver_ref.dtype)
    mirror_energy = jnp.zeros((rows, 1), jnp.float32)
    for i in range(shape.energy):
        width = min(TILE, rows - i * TILE)
        first = (2 * shape.cap + i) * CHUNK
        terms = bundle_ref[first : first + CHUNK, :width].astype(jnp.float32)
        other_energy = (terms[0:1] + terms[1:2]) + terms[2:3]
        here = table[:, i * TILE : i * TILE + width]
        mirror_energy += jnp.where(here, other_energy, 0.0).sum(axis=1, keepdims=True)
    for i, value in enumerate((row_label, column(energy_row[...]), mirror_energy)):
        columns_ref[i * rows : (i + 1) * rows, :] = jnp.broadcast_to(value, (rows, TILE))


def bounds(plan, core, first, count):
    return pl.ds(pl.multiple_of(core * plan.half * TILE + first, TILE), count)


def first_column(plan, place, i):
    here = lax.rem(place[0], plan.near)
    return lax.rem(here + 2 + i, plan.near) * plan.slab * TILE


def slot_of_near(plan, turn):
    return (-(turn // 2 + 1) - 2) % plan.near


def slot_of_far(plan, turn):
    return (-turn - 2) % plan.near


def turns_for(plan, slots):
    return (
        [t for t in range(2 * (plan.near - 1)) if slot_of_near(plan, t) in slots],
        [t for t in range(plan.near) if slot_of_far(plan, t) in slots],
    )


def fill(plan, slots, own, other, place, near_got, far_got, swapped, ints_ref, labels, spots):
    z, side, sub = place[0], place[1], place[2]
    here = lax.rem(z, plan.near)
    ints_ref[...] = jnp.zeros_like(ints_ref)
    all_labels(plan, own, other, sub, labels)
    near_turns, far_turns = turns_for(plan, slots)

    def put(slot, n, value):
        spot = spots[n]
        j, k = split(spot, plan.tiles)
        ints_ref[tile_at(k), tile_at((slot - slots[0]) * plan.slab + j)] = value

    def list_slot(slot):
        slab = sub * plan.near + lax.rem(here + 2 + slot, plan.near)
        list_tiles(plan, labels, slab, spots)

    @pl.when(z // plan.near == sub)
    def _():
        for turn in near_turns:
            slot = slot_of_near(plan, turn)
            if turn % 2 == 0:
                list_slot(slot)
            for n in range(plan.part):
                tile = near_got[turn][n * TILE : (n + 1) * TILE, :]
                put(slot, turn % 2 * plan.part + n, tile)

    @pl.when(z // plan.near != sub)
    def _():
        for turn in far_turns:
            slot = slot_of_far(plan, turn)
            list_slot(slot)
            for n in range(plan.part):
                rows = slice(n * TILE, (n + 1) * TILE)
                put(slot, side * plan.part + n, far_got[turn][rows, :])
                put(slot, (1 - side) * plan.part + n, swapped[turn][rows, :])


def new_current(plan, slots, own, place, pieces, ints_ref, driver, mirror_driver, columns, col_energy,
                cur_ref):
    rows = driver.shape[0]
    width = plan.slab * TILE
    wide = min(width, 2 * TILE)
    terms = []
    for i, piece in enumerate(pieces):
        core = place[2] if i < PIECES else 1 - place[2]
        sizes = [tiles * TILE for tiles in plan.pieces(2 * rows)]
        terms.append((piece, bounds(plan, core, i % PIECES * sizes[0], sizes[i % PIECES])))
    for slot in slots:
        first = first_column(plan, place, slot)
        for c in range(0, width, wide):
            cols = slice((slot - slots[0]) * width + c, (slot - slots[0]) * width + c + wide)
            total = None
            for piece, at in terms:
                term = jnp.dot(piece[...], ints_ref[at, cols], preferred_element_type=jnp.float32)
                total = term if total is None else total + term
            sym = total[:rows] + total[rows:]
            for t in range(0, wide, TILE):
                at = pl.ds(pl.multiple_of(first + c + t, TILE), TILE)
                occupied = columns[:rows] == own[(first + c + t) // TILE].astype(jnp.float32)
                for i, source in enumerate((driver, mirror_driver)):
                    gap = col_energy[:, at] - columns[(i + 1) * rows : (i + 2) * rows]
                    new = (source[:, at].astype(jnp.float32) + sym[:, t : t + TILE]) / gap
                    new = jnp.where(occupied, new, 0.0)
                    cur_ref[i * rows : (i + 1) * rows, cols.start + t : cols.start + t + TILE] = (
                        new.astype(cur_ref.dtype)
                    )


def take_turns(turns, refs):
    refs = list(refs)
    return [{t: refs.pop(0) for t in each} for each in (turns[0], turns[1], turns[1])]


def early_kernel(plan, turns, *refs):
    own, other, place, mine_ref, their_ref = refs[:5]
    pieces, refs = refs[5 : 5 + 2 * PIECES], refs[5 + 2 * PIECES :]
    came = take_turns(turns, refs[4:-4])
    ints_ref, cur_ref, labels, spots = refs[-4:]
    slots = range(plan.near - 1)
    width = plan.slab * TILE
    fill(plan, slots, own, other, place, *came, ints_ref, labels, spots)

    @pl.when(place[0] // plan.near == place[2])
    def _():
        cols = slice((plan.near - 2) * width, (plan.near - 1) * width)
        ints_ref[bounds(plan, place[2], 0, plan.half * TILE), cols] = mine_ref[...]
        ints_ref[bounds(plan, 1 - place[2], 0, plan.half * TILE), cols] = their_ref[...]

    new_current(plan, slots, own, place, pieces, ints_ref, *refs[:4], cur_ref)


def late_kernel(plan, turns, *refs):
    own, other, place = refs[:3]
    pieces, refs = refs[3 : 3 + 2 * PIECES], refs[3 + 2 * PIECES :]
    came = take_turns(turns, refs[4:-4])
    ints_ref, cur_ref, labels, spots = refs[-4:]
    slots = range(plan.near - 1, plan.near)
    fill(plan, slots, own, other, place, *came, ints_ref, labels, spots)
    new_current(plan, slots, own, place, pieces, ints_ref, *refs[:4], cur_ref)


def product(plan, place, terms, ints_ref, cols):
    width = plan.slab * TILE
    total = None
    for cur_ref, core, slots in terms:
        for slot in slots:
            at = slice((slot - slots[0]) * width, (slot - slots[0] + 1) * width)
            rows = bounds(plan, core, first_column(plan, place, slot), width)
            term = jnp.dot(
                cur_ref[:, at], ints_ref[rows, cols], preferred_element_type=jnp.float32
            )
            total = term if total is None else total + term
    half = total.shape[0] // 2
    return total[:half] + total[half:]


def blocks(plan, count):
    width = plan.slab * TILE
    wide = min(width, 2 * TILE)
    return [slice(c, c + wide) for c in range(0, count * width, wide)]


def early_part_kernel(plan, place, a_mine, a_their, ints_a, sym_ref):
    a = range(plan.near - 1)
    terms = [(a_mine, place[2], a), (a_their, 1 - place[2], a)]
    for cols in blocks(plan, plan.near - 1):
        sym_ref[:, cols] = product(plan, place, terms, ints_a, cols)


def part_kernel(plan, place, a_mine, a_their, b_mine, ints_a, ints_b, early_ref, sym_ref):
    a, b = range(plan.near - 1), range(plan.near - 1, plan.near)
    terms = [(b_mine, place[2], b)]
    for cols in blocks(plan, plan.near - 1):
        sym_ref[:, cols] = early_ref[:, cols] + product(plan, place, terms, ints_a, cols)
    terms = [(a_mine, place[2], a), (a_their, 1 - place[2], a), (b_mine, place[2], b)]
    width = (plan.near - 1) * plan.slab * TILE
    for cols in blocks(plan, 1):
        sym_ref[:, width + cols.start : width + cols.stop] = product(plan, place, terms, ints_b, cols)


def last_kernel(plan, own, place, b_their, ints_a, ints_b, sym_ref, driver, columns, col_energy, out_ref,
                new_ref, sems):
    rows = driver.shape[0]
    terms = [(b_their, 1 - place[2], range(plan.near - 1, plan.near))]
    width = plan.slab * TILE
    copies = []
    for c, cols in enumerate(blocks(plan, plan.near)):
        slot = cols.start // width
        ints_ref, start = (ints_b, cols.start - slot * width) if slot == plan.near - 1 else (ints_a, cols.start)
        wide = cols.stop - cols.start
        sym = sym_ref[:, cols] + product(plan, place, terms, ints_ref, slice(start, start + wide))
        first = first_column(plan, place, slot) + cols.start - slot * width
        for t in range(0, wide, TILE):
            at = pl.ds(pl.multiple_of(first + t, TILE), TILE)
            occupied = columns[:rows] == own[(first + t) // TILE].astype(jnp.float32)
            gap = col_energy[:, at] - columns[rows : 2 * rows]
            new = (driver[:, at].astype(jnp.float32) + sym[:, t : t + TILE]) / gap
            new_ref[:, cols.start + t : cols.start + t + TILE] = jnp.where(occupied, new, 0.0)
        at = pl.ds(pl.multiple_of(first, TILE), wide)
        copy = pltpu.make_async_copy(new_ref.at[:, cols], out_ref.at[:, at], sems.at[c])
        copy.start()
        copies.append(copy)
    for copy in copies:
        copy.wait()


def call(kernel, smem, vmem, outs, scratch=(), anywhere=(), flag=False, flops=0, to_hbm=False):
    moved = sum(v.size * v.dtype.itemsize for v in vmem)
    in_smem, in_vmem = pl.BlockSpec(memory_space=pltpu.SMEM), pl.BlockSpec(memory_space=pltpu.VMEM)
    in_any = pl.BlockSpec(memory_space=pl.ANY)
    return pl.pallas_call(
        kernel,
        out_shape=list(outs) + [jax.ShapeDtypeStruct((1,), jnp.int32)] * flag,
        in_specs=[in_smem] * len(smem) + [in_vmem] * len(vmem) + [in_any] * len(anywhere),
        out_specs=[pl.BlockSpec(memory_space=pltpu.HBM) if to_hbm else in_vmem] * len(outs) + [in_smem] * flag,
        scratch_shapes=scratch,
        compiler_params=pltpu.CompilerParams(vmem_limit_bytes=VMEM_BYTES),
        cost_estimate=pl.CostEstimate(flops=0, bytes_accessed=0, transcendentals=0),
    )(*smem, *vmem, *anywhere)


def body(
    amplitudes, driver, integrals, pair_energy, col_energy, tile_irrep, pair_irrep, mirror_slot
):
    places, sides = lax.axis_size("virt"), lax.axis_size("pair")
    partner_bit = sides.bit_length() - 2
    rows, half_cols = amplitudes.shape
    slab_tiles = integrals.shape[1] // TILE
    plans = [
        Plan(2 * half_cols // TILE, slab_tiles, places, per_tile * slab_tiles)
        for per_tile in CAPS
    ]
    plan = plans[-1]
    z, sub = lax.axis_index("virt"), lax.axis_index("sub")
    side = (lax.axis_index("pair") >> partner_bit) & 1
    place = jnp.stack([z, side, sub]).astype(jnp.int32)

    def like(shape, dtype=integrals.dtype):
        return jax.ShapeDtypeStruct(shape, dtype)

    other_irrep = from_partner(tile_irrep, "sub", 0)
    their_ints = from_partner(integrals, "sub", 0)

    label_row, slot_row, energy_row = pair_irrep[None, :], mirror_slot[None, :], pair_energy[None, :]
    shape = Rows(rows, half_cols)
    sort_scratch = [pltpu.VMEM((shape.sorted, half_cols), amplitudes.dtype)] * 2 + [
        pltpu.SMEM((2 * IRREPS,), jnp.int32),
        pltpu.SMEM((shape.tiles * shape.most + 1,), jnp.int32),
    ]
    bundle, rows_full = call(
        functools.partial(rows_kernel, shape),
        (tile_irrep,),
        (amplitudes, driver, label_row, energy_row),
        [like((shape.sent, TILE))],
        sort_scratch,
        flag=True,
    )

    lists = [pltpu.SMEM((plan.tiles,), jnp.int32), pltpu.SMEM((plan.slab * plan.tiles + 1,), jnp.int32)]
    level, spots = list_tiles_of(plans, lists, tile_irrep, other_irrep, place, bundle)

    def sparse(index):
        return sparse_plan(
            plans[index], spots, place, lists, shape, sort_scratch,
            other_irrep, their_ints, bundle, rows_full, amplitudes, driver, integrals, label_row,
            slot_row, energy_row, col_energy, tile_irrep,
        )

    def dense():
        return dense_plan(
            amplitudes, driver, integrals, pair_energy, col_energy, tile_irrep, pair_irrep,
            mirror_slot,
        )

    branches = [functools.partial(sparse, index) for index in range(len(plans))] + [dense]
    return lax.switch(level[0], branches)


def list_tiles_of(plans, lists, own, other, place, after):
    smem = pl.BlockSpec(memory_space=pltpu.SMEM)

    def kernel(own, other, place, after_ref, *refs):
        list_kernel(plans, own, other, place, *refs)

    return pl.pallas_call(
        kernel,
        out_shape=[
            jax.ShapeDtypeStruct((1,), jnp.int32),
            jax.ShapeDtypeStruct((plans[-1].cap,), jnp.int32),
        ],
        in_specs=[smem] * 3 + [pl.BlockSpec(memory_space=pl.ANY)],
        out_specs=[smem] * 2,
        scratch_shapes=lists + [pltpu.SMEM((plans[-1].tiles,), jnp.int32)],
    )(own, other, place, after)


def sparse_plan(
    plan, spots, place, lists, shape, sort_scratch, other_irrep, their_ints, bundle, rows_full,
    amplitudes, driver, integrals, label_row, slot_row, energy_row, col_energy, tile_irrep,
):
    places, sides = lax.axis_size("virt"), lax.axis_size("pair")
    partner_bit = sides.bit_length() - 2
    rows, half_cols = amplitudes.shape

    def like(shape, dtype=integrals.dtype):
        return jax.ShapeDtypeStruct(shape, dtype)

    def over_pair(value):
        return from_partner(value, "pair", partner_bit)

    sends = call(
        functools.partial(pack_kernel, plan),
        (spots, place),
        (integrals, their_ints),
        [like((plan.part * TILE, TILE))] * 2,
    )

    near = plan.near
    got = []
    for turn in range(max(2 * (near - 1), near)):
        pairs = []
        for i in range(places):
            half, at = i // near, i % near
            if turn < 2 * (near - 1):
                to = half * near + (at + turn // 2 + 1) % near
                pairs.append((2 * i + half, 2 * to + half))
            if turn < near:
                to = (1 - half) * near + (at + turn) % near
                pairs.append((2 * i + 1 - half, 2 * to + half))
        got.append(lax.ppermute(sends[turn % 2], ("virt", "sub"), pairs))
    across = []
    for i in range(places):
        for j in range(sides):
            far = 1 - i // near
            across.append(((i * sides + j) * 2 + far, (i * sides + (j ^ 1 << partner_bit)) * 2 + far))
    near_got, far_got = got, got[:near]
    swapped = [lax.ppermute(value, ("virt", "pair", "sub"), across) for value in far_got]

    other_bundle = over_pair(bundle)
    energy = col_energy[None, :]

    def mirror(whole, more=()):
        return tuple(call(
            functools.partial(mirror_kernel, shape, plan.pieces(2 * rows), whole),
            (tile_irrep,),
            (amplitudes, other_bundle, slot_row, label_row, energy_row, *more),
            [like((2 * rows, tiles * TILE)) for tiles in plan.pieces(2 * rows)]
            + [like((rows, half_cols)), like((3 * rows, TILE), jnp.float32)],
            () if whole else sort_scratch,
        ))

    *cur_mine, mirror_driver, columns = lax.cond(
        rows_full[0] > 0,
        lambda: mirror(True, (over_pair(amplitudes), over_pair(driver))),
        lambda: mirror(False),
    )
    cur_their = [from_partner(piece, "sub", 0) for piece in cur_mine]

    width = plan.slab * TILE
    near_cols, flops = (near - 1) * width, 2 * 2 * rows * plan.tiles * TILE * width
    common = (*cur_mine, *cur_their, driver, mirror_driver, columns, energy)

    def came(turns):
        near_turns, far_turns = turns
        values = [near_got[t] for t in near_turns] + [far_got[t] for t in far_turns]
        return values + [swapped[t] for t in far_turns]

    turns = turns_for(plan, range(near - 1))
    ints_a, a_mine = call(
        functools.partial(early_kernel, plan, turns),
        (tile_irrep, other_irrep, place),
        (integrals, their_ints, *common, *came(turns)),
        [like((plan.tiles * TILE, near_cols)), like((2 * rows, near_cols))],
        lists,
        flops=flops * (near - 1),
    )
    a_their = from_partner(a_mine, "sub", 0)
    (early,) = call(
        functools.partial(early_part_kernel, plan),
        (place,),
        (a_mine, a_their, ints_a),
        [like((rows, near_cols), jnp.float32)],
        flops=flops // 2,
    )
    turns = turns_for(plan, range(near - 1, near))
    ints_b, b_mine = call(
        functools.partial(late_kernel, plan, turns),
        (tile_irrep, other_irrep, place),
        (*common, *came(turns)),
        [like((plan.tiles * TILE, width)), like((2 * rows, width))],
        lists,
        flops=flops,
    )
    b_their = from_partner(b_mine, "sub", 0)
    (sym,) = call(
        functools.partial(part_kernel, plan),
        (place,),
        (a_mine, a_their, b_mine, ints_a, ints_b, early),
        [like((rows, half_cols), jnp.float32)],
        flops=flops,
    )
    return call(
        functools.partial(last_kernel, plan),
        (tile_irrep, place),
        (b_their, ints_a, ints_b, sym, driver, columns, energy),
        [like((rows, half_cols), jnp.float32)],
        [pltpu.VMEM((rows, half_cols), jnp.float32),
         pltpu.SemaphoreType.DMA((len(blocks(plan, near)),))],
        flops=flops // 2,
        to_hbm=True,
    )[0]


def solution(mesh):
    return jax.shard_map(
        body,
        mesh=mesh,
        in_specs=(
            P(("groups", "pair", "virt"), "sub"),
            P(("groups", "pair", "virt"), "sub"),
            P(("groups", "sub"), "virt"),
            P(("groups", "pair", "virt")),
            P(("groups", "sub")),
            P(("groups", "sub")),
            P(("groups", "pair", "virt")),
            P(("groups", "pair", "virt")),
        ),
        out_specs=P(("groups", "pair", "virt"), "sub"),
        check_vma=False,
    )
```
